128 devices in a mesh: lat: 8 (over x_hi, y), lon: 16 (over z, x_lo, core).
Axes of the slice: x: 4 (x_hi: 2, x_lo: 2; x = x_hi * 2 + x_lo), y: 4, z: 4, core: 2. Of those that a mesh axis runs over, the one named last changes fastest.
Arguments:
- latent: bfloat16 [2, 192, 768, 512], P(None, 'lat', 'lon'), may hold values from -6 to 6
- cotangent: bfloat16 [2, 192, 768, 512], P(None, 'lat', 'lon'), may hold values from -6 to 6
- qkv_weight: bfloat16 [512, 1536], P(('lat', 'lon')), may hold values from -2 to 2
- out_weight: bfloat16 [512, 512], P(('lat', 'lon')), may hold values from -0.25 to 0.25
Outputs:
- output: bfloat16 [2, 192, 768, 512], P(None, 'lat', 'lon')
- grad_latent: bfloat16 [2, 192, 768, 512], P(None, 'lat', 'lon')
- grad_qkv: float32 [512, 1536], P(('lat', 'lon'))
- grad_out_weight: float32 [512, 512], P(('lat', 'lon'))
The draws below stay inside these ranges and needn't reach their ends.
All inputs are finite; a program needn't handle non-finite values.
Results may differ from the reference program's by a relative error of at most 0.013.
Values may be sent and summed in bfloat16 or wider, within the bound.
A program may use at most 128 MiB of HBM per device.

```python
import math
import jax
import jax.numpy as jnp
from jax import lax

C = 512
HEADS = 8
HD = 64
LEV = 2
WIN_LAT = 6
WIN_LON = 12
H = 192
W = 768
TOKENS = 294912


def draw_qkv_weight(key, part):
    key = jax.random.fold_in(key, 11)
    key_base = jax.random.fold_in(key, 0)
    drawn = jax.random.normal(key_base, (C, 3 * C), jnp.float32) * C ** (-0.5)
    return jnp.clip(drawn, -2.0, 2.0).astype(jnp.bfloat16)


def steps_of(stream_key, dims, cuts, smallest, high):
    gain, own = 1.0, jax.random.fold_in(stream_key, 6)
    for position, blocks in cuts:
        heights = jnp.exp(jax.random.uniform(jax.random.fold_in(own, position), (blocks,), jnp.float32, smallest / len(cuts), high / len(cuts)))
        gain = gain * jnp.repeat(heights, dims[position] // blocks).reshape([-1 if axis == position else 1 for axis in range(len(dims))])
    return gain


def bell_draw(key, shape, deviation, limit, cuts=(), kind=jnp.bfloat16):
    entries = jax.random.normal(key, shape, jnp.float32) * deviation
    if len(cuts) > 0:
        entries = steps_of(key, shape, cuts, -0.22, 0.18) * entries
    return jnp.clip(entries, min=-limit, max=limit).astype(kind)


def setup_inputs(seed: int = 0) -> dict:
    seeds = jax.random.split(jax.random.key(seed), 5)
    return {
        "latent": bell_draw(seeds[0], (LEV, H, W, C), 1.0, 6.0, ((1, 8), (2, 16))),
        "cotangent": bell_draw(seeds[1], (LEV, H, W, C), 1.0, 6.0, ((1, 8), (2, 16))),
        "qkv_weight": draw_qkv_weight(jax.random.fold_in(seeds[4], 71), 0),
        "out_weight": bell_draw(seeds[3], (C, C), C ** -0.5, 0.25, ((0, 128),)),
    }


def product(pattern, left, right):
    left, right = lax.optimization_barrier((left, right))
    return jnp.einsum(pattern, left.astype(jnp.float32), right.astype(jnp.float32))

def matmul(left, right):
    return jnp.dot(left, right, preferred_element_type=jnp.float32)

def times_transposed(left, right):
    return lax.dot_general(left, right, (((1,), (1,)), ((), ())), preferred_element_type=jnp.float32)

def transposed_times(left, right):
    return lax.dot_general(left, right, (((0,), (0,)), ((), ())), preferred_element_type=jnp.float32)

def windowed(grid_block):
    levels, row_count, columns, features = grid_block.shape
    pieces = grid_block.reshape(levels, row_count, columns // WIN_LON, WIN_LON, features)
    return pieces.transpose(2, 0, 1, 3, 4).reshape(columns // WIN_LON, levels * row_count * WIN_LON, features)

def unwindowed(window_tiles, levels, row_count):
    window_count, tokens, features = window_tiles.shape
    pieces = window_tiles.reshape(window_count, levels, row_count, WIN_LON, features)
    return pieces.transpose(1, 2, 0, 3, 4).reshape(levels, row_count, window_count * WIN_LON, features)

def to_slabs(grid_block):
    levels, row_count, columns, features = grid_block.shape
    pieces = grid_block.reshape(levels, row_count // WIN_LAT, WIN_LAT, columns, features)
    return pieces.transpose(1, 0, 2, 3, 4)

def from_slabs(stacked):
    slab_count, levels, row_count, columns, features = stacked.shape
    return stacked.transpose(1, 0, 2, 3, 4).reshape(levels, slab_count * row_count, columns, features)

def slab_step(qkv_weight, out_weight, inputs):
    rolled_slab, cot_slab, flag_row = inputs
    levels, row_count, columns, features = rolled_slab.shape
    score_scale = HD ** (-0.5)
    tiles = windowed(rolled_slab)
    window_count, tokens = (tiles.shape[0], tiles.shape[1])
    widened = tiles.reshape(-1, C).astype(jnp.float32)
    centred = widened - lax.optimization_barrier(jnp.mean(widened, -1, keepdims=True))
    inv_scale = lax.rsqrt(lax.optimization_barrier(jnp.mean(centred * centred, -1, keepdims=True)) + 1e-05)
    standard = centred * inv_scale
    normed = standard.astype(jnp.bfloat16)
    projections = matmul(normed, qkv_weight).astype(jnp.bfloat16)
    queries = projections[:, :C].reshape(window_count, tokens, HEADS, HD)
    key_heads = projections[:, C:2 * C].reshape(window_count, tokens, HEADS, HD)
    values = projections[:, 2 * C:].reshape(window_count, tokens, HEADS, HD)
    flag_full = jnp.broadcast_to(flag_row[None, :, None, None], (levels, row_count, columns, 1))
    flag_tiles = windowed(flag_full)[:, :, 0]
    allowed = flag_tiles[:, None, :, None] == flag_tiles[:, None, None, :]
    scores = product('wqhd,wkhd->whqk', queries, key_heads) * score_scale
    scores = jnp.where(allowed, scores, -1e+30)
    maximum = lax.optimization_barrier(jnp.max(scores, -1, keepdims=True))
    shifted_exp = jnp.exp(scores - maximum)
    attention = shifted_exp / lax.optimization_barrier(jnp.sum(shifted_exp, -1, keepdims=True))
    attention_low = attention.astype(jnp.bfloat16)
    context = product('whqk,wkhd->wqhd', attention_low, values).astype(jnp.bfloat16).reshape(-1, C)
    result = (widened + matmul(context, out_weight)).astype(jnp.bfloat16)
    incoming = windowed(cot_slab).reshape(-1, C)
    grad_context = times_transposed(incoming, out_weight).astype(jnp.bfloat16)
    out_term = transposed_times(context, incoming)
    context_heads = grad_context.reshape(window_count, tokens, HEADS, HD)
    grad_attention = product('wqhd,wkhd->whqk', context_heads, values)
    grad_values = product('whqk,wqhd->wkhd', attention_low, context_heads).astype(jnp.bfloat16)
    inner = lax.optimization_barrier(jnp.sum(grad_attention * attention, -1, keepdims=True))
    grad_scores = (attention * (grad_attention - inner) * score_scale).astype(jnp.bfloat16)
    grad_queries = product('whqk,wkhd->wqhd', grad_scores, key_heads).astype(jnp.bfloat16)
    grad_keys = product('whqk,wqhd->wkhd', grad_scores, queries).astype(jnp.bfloat16)
    grad_packed = jnp.concatenate([grad_queries.reshape(-1, C), grad_keys.reshape(-1, C), grad_values.reshape(-1, C)], 1)
    qkv_term = transposed_times(normed, grad_packed)
    grad_normed = times_transposed(grad_packed, qkv_weight)
    first_mean = lax.optimization_barrier(jnp.mean(grad_normed, -1, keepdims=True))
    second_mean = lax.optimization_barrier(jnp.mean(grad_normed * standard, -1, keepdims=True))
    grad_input = inv_scale * (grad_normed - first_mean - standard * second_mean) + incoming.astype(jnp.float32)
    grad_input = grad_input.astype(jnp.bfloat16)
    result_grid = unwindowed(result.reshape(window_count, tokens, C), levels, row_count)
    grad_grid = unwindowed(grad_input.reshape(window_count, tokens, C), levels, row_count)
    return (result_grid, grad_grid, qkv_term, out_term)

def run_layer(rolled, rolled_cot, row_flags, qkv_weight, out_weight):
    row_count = rolled.shape[1]
    flag_rows = row_flags.reshape(row_count // WIN_LAT, WIN_LAT)

    def advance(totals, inputs):
        result, grad_input, qkv_term, out_term = slab_step(qkv_weight, out_weight, inputs)
        return ((totals[0] + qkv_term, totals[1] + out_term), (result, grad_input))
    initial = (jnp.zeros((C, 3 * C), jnp.float32), jnp.zeros((C, C), jnp.float32))
    totals, outputs = lax.scan(advance, initial, (to_slabs(rolled), to_slabs(rolled_cot), flag_rows))
    return (from_slabs(outputs[0]), from_slabs(outputs[1]), totals[0], totals[1])

def reference(latent, cotangent, qkv_weight, out_weight):
    half_rows = WIN_LAT // 2
    half_cols = WIN_LON // 2
    rolled = jnp.roll(latent, (-half_rows, -half_cols), axis=(1, 2))
    rolled_cot = jnp.roll(cotangent, (-half_rows, -half_cols), axis=(1, 2))
    row_flags = jnp.arange(H, dtype=jnp.int32) >= H - half_rows
    result, grad_input, qkv_term, out_term = run_layer(rolled, rolled_cot, row_flags, qkv_weight, out_weight)
    output = jnp.roll(result, (half_rows, half_cols), axis=(1, 2))
    grad_latent = jnp.roll(grad_input, (half_rows, half_cols), axis=(1, 2))
    factor = 1.0 / math.sqrt(TOKENS)
    return (output, grad_latent, qkv_term * factor, out_term * factor)
```

```python
import functools
import math

import jax
import jax.numpy as jnp
from jax import lax
from jax.experimental import pallas as pl
from jax.experimental.pallas import tpu as pltpu
from jax.sharding import PartitionSpec as P

C = 512
HD = 64
WIN_LAT = 6
WIN_LON = 12
LEVELS = 2
PIECES = LEVELS * WIN_LAT
TOK = PIECES * WIN_LON
SLABS = 4
ACROSS = 4
WINDOWS = SLABS * ACROSS
TOKENS = WINDOWS * TOK
CHUNK = 2 * ACROSS * TOK
HALF_ROWS = 3
HALF_COLS = 6
ROWS = 24
COLS = 48
TILES = 13
BF = jnp.bfloat16
F32 = jnp.float32


def nn(a, b):
    return lax.dot_general(a, b, (((1,), (0,)), ((), ())), preferred_element_type=F32)


def nt(a, b):
    return lax.dot_general(a, b, (((1,), (1,)), ((), ())), preferred_element_type=F32)


def tn(a, b):
    return lax.dot_general(a, b, (((0,), (0,)), ((), ())), preferred_element_type=F32)


def halo_tile(slab, row):
    if isinstance(slab, int) and slab == SLABS - 1 and row >= HALF_ROWS:
        return 11 + (row - HALF_ROWS) // 2, (row - HALF_ROWS) % 2
    return 3 * slab + row // 2, row % 2


def layer_kernel(
    lat_ref, cot_ref, hr_ref, hc_ref, w_ref,
    out_ref, grad_ref, rr_ref, rc_ref, dw_ref,
    rows, window, wide, x_w, cot_w, inv_w, normed, normed_t, ctx, ctx_t, gctx, qkv, gp, bias, bias_tail,
):
    last = lax.axis_index("lat") == lax.axis_size("lat") - 1

    key = lax.broadcasted_iota(jnp.int32, (TOK, 128), 0)
    query = lax.broadcasted_iota(jnp.int32, (TOK, 128), 1)

    def flag(token):
        row = token // WIN_LON
        return jnp.where(row >= WIN_LAT, row - WIN_LAT, row) >= HALF_ROWS

    seam = jnp.where(last, -1e30, 0.0).astype(F32)
    bias[0] = jnp.zeros((TOK, 128), F32)
    bias_tail[0] = jnp.zeros((TOK, 128), F32)
    bias[1] = jnp.where(flag(key) != flag(query), seam, 0.0)
    bias_tail[1] = jnp.where(flag(key), 0.0, seam)

    def load_slab(slab):
        for which, source in enumerate((lat_ref, cot_ref)):
            for level in range(LEVELS):
                for row in range(WIN_LAT):
                    piece = level * WIN_LAT + row
                    if isinstance(slab, int) and slab == SLABS - 1 and row >= HALF_ROWS:
                        own = hr_ref[which, level, row - HALF_ROWS]
                    else:
                        own = source[level, slab * WIN_LAT + row + HALF_ROWS]
                    rows[which, piece, :COLS] = own.astype(F32)
                    tile, half = halo_tile(slab, row)
                    rows[which, piece, COLS:] = hc_ref[which, level, tile].astype(F32)[8 * half : 8 * half + 8]
        for across in range(ACROSS):
            start = HALF_COLS + WIN_LON * across
            token = pl.multiple_of((slab * ACROSS + across) * TOK, 16)
            for which in range(2):
                for piece in range(PIECES):
                    window[which, WIN_LON * piece : WIN_LON * (piece + 1)] = rows[which, piece, start : start + WIN_LON]
            widened = window[0]
            centred = widened - jnp.mean(widened, -1, keepdims=True)
            inv = lax.rsqrt(jnp.mean(centred * centred, -1, keepdims=True) + 1e-05)
            x_w[pl.ds(token, TOK)] = widened.astype(BF)
            inv_w[pl.ds(token, TOK)] = inv
            normed[pl.ds(token, TOK)] = (centred * inv).astype(BF)
            cot_w[pl.ds(token, TOK)] = window[1].astype(BF)

    pl.loop(0, SLABS - 1)(load_slab)
    load_slab(SLABS - 1)

    def project(chunk):
        part = pl.ds(pl.multiple_of(chunk * CHUNK, 128), CHUNK)
        block = normed[part]
        for third in range(3):
            cols = slice(C * third, C * (third + 1))
            made = nn(block, w_ref[:, cols]).astype(BF)
            qkv[part, cols] = made * BF(HD ** -0.5) if third == 0 else made
        gctx[part] = nt(cot_w[part], w_ref[:, 3 * C :]).astype(BF)
        normed_t[:, part] = block.T

    pl.loop(0, TOKENS // CHUNK)(project)

    lane = lax.broadcasted_iota(jnp.int32, (1, 128), 1)
    low = (lane < HD).astype(F32).astype(BF)
    high = (lane >= HD).astype(F32).astype(BF)
    low_lanes = lax.broadcasted_iota(jnp.int32, (128, 128), 1) < HD
    low_lanes16 = lax.broadcasted_iota(jnp.int32, (16, 128), 1) < HD

    def spread(tail):
        zero = jnp.zeros((16, 128), BF)
        lines = []
        for head in range(8):
            pair = head // 2
            mine = tail[:, 128 * pair : 128 * (pair + 1)] * (low if head % 2 == 0 else high)
            lines.append(jnp.concatenate([mine if p == pair else zero for p in range(4)], 1))
        return jnp.concatenate(lines, 0)

    def gather(full, pair):
        cols = slice(128 * pair, 128 * (pair + 1))
        return jnp.where(low_lanes16, full[32 * pair : 32 * pair + 16, cols], full[32 * pair + 16 : 32 * pair + 32, cols])

    def softmax_both(scores, grad_att):
        top = jnp.max(scores, 0, keepdims=True)
        raised = jnp.exp(scores - top)
        att = raised * (1.0 / jnp.sum(raised, 0, keepdims=True))
        weighed = grad_att * att
        inner = jnp.sum(weighed, 0, keepdims=True)
        return att.astype(BF), (weighed - att * inner).astype(BF)

    @pl.loop(0, WINDOWS)
    def _(win):
        token = pl.multiple_of(win * TOK, 16)
        seam_slab = (win >= WINDOWS - ACROSS).astype(jnp.int32)
        main = pl.ds(token, 128)
        tail = pl.ds(pl.multiple_of(token + 128, 16), 16)
        whole = pl.ds(token, TOK)
        q_tail = spread(qkv[tail, :C])
        g_tail = spread(gctx[tail])
        keys = qkv[whole, C : 2 * C]
        values = qkv[whole, 2 * C :]
        att_t, gs_t = softmax_both(nt(keys, q_tail) + bias_tail[seam_slab], nt(values, g_tail))
        ctx_tail = tn(att_t, values)
        gq_tail = tn(gs_t, keys)
        gk_tail = nn(gs_t, q_tail)
        gv_tail = nn(att_t, g_tail)
        offset = bias[seam_slab]
        offset = jnp.concatenate([offset, offset], 1)
        for pair in range(4):
            cols = slice(128 * pair, 128 * (pair + 1))
            q = qkv[main, cols]
            g = gctx[main, cols]
            q_both = jnp.concatenate([q * low, q * high], 0)
            g_both = jnp.concatenate([g * low, g * high], 0)
            k = keys[:, cols]
            v = values[:, cols]
            att, gs = softmax_both(nt(k, q_both) + offset, nt(v, g_both))
            made = tn(att, v)
            ctx[main, cols] = jnp.where(low_lanes, made[:128], made[128:]).astype(BF)
            ctx[tail, cols] = gather(ctx_tail, pair).astype(BF)
            gq = tn(gs, k)
            gp[main, cols] = (jnp.where(low_lanes, gq[:128], gq[128:]) * HD ** -0.5).astype(BF)
            gp[tail, cols] = (gather(gq_tail, pair) * HD ** -0.5).astype(BF)
            gp[whole, C + 128 * pair : C + 128 * (pair + 1)] = (nn(gs, q_both) + gk_tail[:, cols]).astype(BF)
            gp[whole, 2 * C + 128 * pair : 2 * C + 128 * (pair + 1)] = (nn(att, g_both) + gv_tail[:, cols]).astype(BF)

    def store_slab(slab, first):
        for which, target in enumerate((out_ref, grad_ref)):
            for level in range(LEVELS):
                for row in range(WIN_LAT):
                    piece = level * WIN_LAT + row
                    for across in range(ACROSS):
                        start = HALF_COLS + WIN_LON * across
                        rows[which, piece, start : start + WIN_LON] = wide[
                            which, pl.ds(first + across * TOK + piece * WIN_LON, WIN_LON)]
                    own = rows[which, piece, :COLS].astype(BF)
                    if isinstance(slab, int) and slab == SLABS - 1 and row >= HALF_ROWS:
                        rr_ref[which, level, row - HALF_ROWS] = own
                    else:
                        target[level, slab * WIN_LAT + row + HALF_ROWS] = own
        for which in range(2):
            for level in range(LEVELS):
                for row in range(WIN_LAT):
                    tile, half = halo_tile(slab, row)
                    if half == 1:
                        continue
                    piece = level * WIN_LAT + row
                    more = min(piece + 1, PIECES - 1)
                    rc_ref[which, level, tile] = jnp.concatenate(
                        [rows[which, piece, COLS:], rows[which, more, COLS:]], 0).astype(BF)

    def finish(chunk):
        part = pl.ds(chunk * CHUNK if isinstance(chunk, int) else pl.multiple_of(chunk * CHUNK, 128), CHUNK)
        context = ctx[part]
        ctx_t[:, part] = context.T
        wide[0] = x_w[part].astype(F32) + nn(context, w_ref[:, 3 * C :])
        grad_normed = nt(gp[part], w_ref[:, : 3 * C])
        standard = normed[part].astype(F32)
        first_mean = jnp.mean(grad_normed, -1, keepdims=True)
        second_mean = jnp.mean(grad_normed * standard, -1, keepdims=True)
        wide[1] = inv_w[part] * (grad_normed - first_mean - standard * second_mean) + cot_w[part].astype(F32)

    finish(0)
    store_slab(0, 0)
    store_slab(1, ACROSS * TOK)
    finish(1)
    store_slab(2, 0)
    store_slab(3, ACROSS * TOK)

    for level in range(LEVELS):
        for row in range(HALF_ROWS):
            out_ref[level, row] = jnp.zeros((COLS, C), BF)
            grad_ref[level, row] = jnp.zeros((COLS, C), BF)

    for third in range(3):
        cols = slice(C * third, C * (third + 1))
        dw_ref[:, cols] = nn(normed_t[...], gp[:, cols]).astype(BF)
    dw_ref[:, 3 * C :] = nn(ctx_t[...], cot_w[...]).astype(BF)


def layer(latent, cotangent, row_strip, col_strip, weights):
    grid_shape = jax.ShapeDtypeStruct((LEVELS, ROWS, COLS, C), BF)
    whole = pl.BlockSpec(memory_space=pltpu.VMEM)
    return pl.pallas_call(
        layer_kernel,
        out_shape=(
            grid_shape,
            grid_shape,
            jax.ShapeDtypeStruct((2, LEVELS, HALF_ROWS, COLS, C), BF),
            jax.ShapeDtypeStruct((2, LEVELS, TILES, 16, C), BF),
            jax.ShapeDtypeStruct((C, 4 * C), BF),
        ),
        in_specs=[whole] * 5,
        out_specs=(whole,) * 5,
        scratch_shapes=[
            pltpu.VMEM((2, PIECES, COLS + 8, C), F32),
            pltpu.VMEM((2, TOK, C), F32),
            pltpu.VMEM((2, CHUNK, C), F32),
            pltpu.VMEM((TOKENS, C), BF),
            pltpu.VMEM((TOKENS, C), BF),
            pltpu.VMEM((TOKENS, 1), F32),
            pltpu.VMEM((TOKENS, C), BF),
            pltpu.VMEM((C, TOKENS), BF),
            pltpu.VMEM((TOKENS, C), BF),
            pltpu.VMEM((C, TOKENS), BF),
            pltpu.VMEM((TOKENS, C), BF),
            pltpu.VMEM((TOKENS, 3 * C), BF),
            pltpu.VMEM((TOKENS, 3 * C), BF),
            pltpu.VMEM((2, TOK, 128), F32),
            pltpu.VMEM((2, TOK, 128), F32),
        ],
        compiler_params=pltpu.CompilerParams(vmem_limit_bytes=63 * 2**20),
        name="layer",
    )(latent, cotangent, row_strip, col_strip, weights)
MESH = pl.DeviceIdType.MESH
HALF = 2 * C
GROUP = [(a, b, c) for a in range(2) for b in range(2) for c in range(2)][1:]


class Place:
    def __init__(self):
        self.lat, self.lon = lax.axis_index("lat"), lax.axis_index("lon")
        self.x_hi, self.y = self.lat // 4, self.lat % 4
        self.z, self.x_lo, self.core = self.lon // 4, (self.lon // 2) % 2, self.lon % 2

    def mate(self, flips):
        a, b, c = (v + f - 2 * v * f for v, f in zip((self.x_hi, self.x_lo, self.core), flips))
        return (a * 4 + self.y, self.z * 4 + b * 2 + c)

    def along(self, axis, step):
        if axis == "y":
            return (self.x_hi * 4 + (self.y + step) % 4, self.lon)
        return (self.lat, (self.z + step) % 4 * 4 + self.lon % 4)

    def shifted(self, rows, cols):
        return ((self.lat + rows + 8) % 8, (self.lon + cols + 16) % 16)


def greet(senders):
    barrier = pltpu.get_barrier_semaphore()
    for device in senders:
        pl.semaphore_signal(barrier, inc=1, device_id=device, device_id_type=MESH)
    pl.semaphore_wait(barrier, len(senders))


def remote(src, dst, sems, slot, device):
    return pltpu.make_async_remote_copy(
        src_ref=src, dst_ref=dst, send_sem=sems.at[0, slot], recv_sem=sems.at[1, slot],
        device_id=device, device_id_type=MESH)


def partners(place):
    return ([place.mate(f) for f in GROUP]
            + [place.along("y", s) for s in (1, 2, 3)] + [place.along("z", s) for s in (1, 2, 3)])


def gather_kernel(
    lat_ref, cot_ref, shard_ref,
    hr_ref, hc_ref, w_ref,
    edge, strip, got, loose, edge_sem, halo_sems, group_sems, axis_sems,
):
    place = Place()
    loads = [pltpu.make_async_copy(ref.at[:, :, :16], edge.at[i], edge_sem.at[i])
             for i, ref in enumerate((lat_ref, cot_ref))]
    for load in loads:
        load.start()
    greet(partners(place) + [place.shifted(1, 0), place.shifted(0, 1), place.shifted(1, 1)])
    up, left, corner = place.shifted(-1, 0), place.shifted(0, -1), place.shifted(-1, -1)

    here = (place.x_hi, place.x_lo, place.core)
    group = []
    for slot, flips in enumerate(GROUP):
        copy = remote(shard_ref.at[place.core if flips[2] == 0 else 1 - place.core],
                      got.at[here], group_sems, slot, place.mate(flips))
        copy.start()
        group.append(copy)
    halos = []
    for which, ref in enumerate((lat_ref, cot_ref)):
        for level in range(LEVELS):
            halos.append(remote(ref.at[level, :HALF_ROWS], hr_ref.at[which, level], halo_sems, len(halos), up))
            halos[-1].start()
    got[here] = shard_ref[place.core]

    for which in range(2):
        loads[which].wait()
        for level in range(LEVELS):
            def columns(row):
                return edge[which, level, row].astype(F32)[:8]
            for tile in range(TILES):
                first = HALF_ROWS + 2 * tile if tile < 11 else 2 * (tile - 11)
                end = ROWS if tile < 11 else HALF_ROWS
                pieces = [columns(first), columns(min(first + 1, end - 1))]
                strip[which, level, tile] = jnp.concatenate(pieces, 0).astype(BF)
        halos.append(remote(strip.at[which, :, :11], hc_ref.at[which, :, :11], halo_sems, len(halos), left))
        halos[-1].start()
        halos.append(remote(strip.at[which, :, 11:], hc_ref.at[which, :, 11:], halo_sems, len(halos), corner))
        halos[-1].start()

    for copy in group:
        copy.wait()
    for x_hi in range(2):
        for b in range(2):
            for c in range(2):
                for lane_tile in range(2):
                    line = 16 * (2 * b + c)
                    loose[x_hi, lane_tile, line : line + 16] = got[x_hi, b, c][:, 128 * lane_tile : 128 * lane_tile + 128].astype(F32)
    for core in range(2):
        half = slice(HALF * core, HALF * (core + 1))

        @pl.when(place.core == core)
        def _():
            for x_hi in range(2):
                for block in range(4):
                    for lane_tile in range(2):
                        start = HALF * core + 256 * block + 128 * lane_tile
                        w_ref[x_hi, place.y, place.z, :, start : start + 128] = (
                            loose[x_hi, lane_tile, pl.ds(block, 16, stride=4)].astype(BF))
            first, second = ("z", "y") if core == 0 else ("y", "z")
            small = w_ref.at[:, place.y, place.z, :, half]
            big = w_ref.at[:, place.y, :, :, half] if core == 0 else w_ref.at[:, :, place.z, :, half]
            for stage, (axis, block) in enumerate(((first, small), (second, big))):
                copies = [remote(block, block, axis_sems, 3 * stage + step - 1, place.along(axis, step))
                          for step in (1, 2, 3)]
                for copy in copies:
                    copy.start()
                for copy in copies:
                    copy.wait()
            block = w_ref.at[:, :, :, :, half]
            copy = remote(block, block, axis_sems, 6, place.mate((0, 0, 1)))
            copy.start()
            copy.wait()
    for copy in halos:
        copy.wait()


def gather(latent, cotangent, shard):
    anywhere = pl.BlockSpec(memory_space=pl.ANY)
    whole = pl.BlockSpec(memory_space=pltpu.VMEM)
    return pl.pallas_call(
        gather_kernel,
        out_shape=(
            jax.ShapeDtypeStruct((2, LEVELS, HALF_ROWS, COLS, C), BF),
            jax.ShapeDtypeStruct((2, LEVELS, TILES, 16, C), BF),
            jax.ShapeDtypeStruct((2, 4, 4, 16, 4 * C), BF),
        ),
        in_specs=[anywhere, anywhere, whole],
        out_specs=(anywhere, anywhere, whole),
        scratch_shapes=[
            pltpu.VMEM((2, LEVELS, ROWS, 16, C), BF),
            pltpu.VMEM((2, LEVELS, TILES, 16, C), BF),
            pltpu.VMEM((2, 2, 2, 16, 256), BF),
            pltpu.VMEM((2, 2, 64, 128), F32),
            pltpu.SemaphoreType.DMA((2,)),
            pltpu.SemaphoreType.DMA((2, 8)),
            pltpu.SemaphoreType.DMA((2, 7)),
            pltpu.SemaphoreType.DMA((2, 7)),
        ],
        compiler_params=pltpu.CompilerParams(
            collective_id=0, has_side_effects=True, vmem_limit_bytes=32 * 2**20),
        name="gather",
    )(latent, cotangent, shard)


def reduce_kernel(
    factor,
    rr_ref, rc_ref, dw_ref,
    hr_ref, hc_ref, sums_ref,
    from_mate, total, sent, from_first, total2, sent2, from_second, sent3, from_group,
    halo_sems, axis_sems, group_sems,
):
    place = Place()
    greet(partners(place) + [place.shifted(-1, 0), place.shifted(0, -1), place.shifted(-1, -1)])
    down, right, corner = place.shifted(1, 0), place.shifted(0, 1), place.shifted(1, 1)
    theirs = pl.ds(pl.multiple_of((1 - place.core) * HALF, HALF), HALF)
    mate = remote(dw_ref.at[:, :, :, :, theirs], from_mate, axis_sems, 6, place.mate((0, 0, 1)))
    mate.start()
    halos = []
    for which in range(2):
        halos.append(remote(rr_ref.at[which], hr_ref.at[which], halo_sems, len(halos), down))
        halos.append(remote(rc_ref.at[which, :, :11], hc_ref.at[which, :, :11], halo_sems, len(halos), right))
        halos.append(remote(rc_ref.at[which, :, 11:], hc_ref.at[which, :, 11:], halo_sems, len(halos), corner))
    for copy in halos:
        copy.start()
    mate.wait()
    for core in range(2):
        half = slice(HALF * core, HALF * (core + 1))

        @pl.when(place.core == core)
        def _():
            @pl.loop(0, 8)
            def _(i):
                x_hi, y = i // 4, i % 4
                added = dw_ref[x_hi, y, :, :, half].astype(F32) + from_mate[x_hi, y].astype(F32)
                total[x_hi, y] = added
                sent[x_hi, y] = added.astype(BF)

            first, second = ("y", "z") if core == 0 else ("z", "y")
            copies = []
            for step in (1, 2, 3):
                theirs = (place.y + step) % 4 if core == 0 else (place.z + step) % 4
                block = sent.at[:, theirs] if core == 0 else sent.at[:, :, theirs]
                copies.append(remote(block, from_first.at[step - 1], axis_sems, step - 1, place.along(first, step)))
            for copy in copies:
                copy.start()
            for copy in copies:
                copy.wait()
            for x_hi in range(2):
                mine = total[x_hi, place.y] if core == 0 else total[x_hi, :, place.z]
                added = mine
                for step in range(3):
                    added = added + from_first[step, x_hi].astype(F32)
                total2[x_hi] = added
                sent2[x_hi] = added.astype(BF)
            copies = []
            for step in (1, 2, 3):
                theirs = (place.z + step) % 4 if core == 0 else (place.y + step) % 4
                copies.append(remote(sent2.at[:, theirs], from_second.at[step - 1], axis_sems, 3 + step - 1,
                                     place.along(second, step)))
            for copy in copies:
                copy.start()
            for copy in copies:
                copy.wait()
            added = total2[:, place.z if core == 0 else place.y]
            for step in range(3):
                added = added + from_second[step].astype(F32)
            sent3[...] = added.astype(BF)

    here = (place.x_hi, place.x_lo, place.core)
    copies = []
    for slot, flips in enumerate(GROUP):
        target = place.x_hi if flips[0] == 0 else 1 - place.x_hi
        copies.append(remote(sent3.at[target], from_group.at[here], group_sems, slot, place.mate(flips)))
    for copy in copies:
        copy.start()
    from_group[here] = sent3[place.x_hi]
    for copy in copies:
        copy.wait()
    position = place.x_lo * 2 + place.core
    for core in range(2):
        added = from_group[0, 0, core].astype(F32)
        for a, b in ((0, 1), (1, 0), (1, 1)):
            added = added + from_group[a, b, core].astype(F32)
        picked = added[:4]
        for i in range(1, 4):
            picked = jnp.where(position == i, added[4 * i : 4 * i + 4], picked)
        sums_ref[:, HALF * core : HALF * (core + 1)] = picked * factor
    for copy in halos:
        copy.wait()


def reduce(row_strip, col_strip, dw, factor):
    anywhere = pl.BlockSpec(memory_space=pl.ANY)
    whole = pl.BlockSpec(memory_space=pltpu.VMEM)
    return pl.pallas_call(
        functools.partial(reduce_kernel, factor),
        out_shape=(
            jax.ShapeDtypeStruct((2, LEVELS, HALF_ROWS, COLS, C), BF),
            jax.ShapeDtypeStruct((2, LEVELS, TILES, 16, C), BF),
            jax.ShapeDtypeStruct((4, 4 * C), F32),
        ),
        in_specs=[anywhere, anywhere, whole],
        out_specs=(anywhere, anywhere, whole),
        scratch_shapes=[
            pltpu.VMEM((2, 4, 4, 16, HALF), BF),
            pltpu.VMEM((2, 4, 4, 16, HALF), F32),
            pltpu.VMEM((2, 4, 4, 16, HALF), BF),
            pltpu.VMEM((3, 2, 4, 16, HALF), BF),
            pltpu.VMEM((2, 4, 16, HALF), F32),
            pltpu.VMEM((2, 4, 16, HALF), BF),
            pltpu.VMEM((3, 2, 16, HALF), BF),
            pltpu.VMEM((2, 16, HALF), BF),
            pltpu.VMEM((2, 2, 2, 16, HALF), BF),
            pltpu.SemaphoreType.DMA((2, 6)),
            pltpu.SemaphoreType.DMA((2, 7)),
            pltpu.SemaphoreType.DMA((2, 7)),
        ],
        compiler_params=pltpu.CompilerParams(
            collective_id=1, has_side_effects=True, vmem_limit_bytes=48 * 2**20),
        name="reduce",
    )(row_strip, col_strip, dw)


def merge_kernel(out_in, grad_in, hr_ref, hc_ref, out_ref, grad_ref, edge, top, sems):
    del out_in, grad_in
    outs = (out_ref, grad_ref)
    loads = [pltpu.make_async_copy(ref.at[:, HALF_ROWS:, :16], edge.at[i], sems.at[i]) for i, ref in enumerate(outs)]
    for load in loads:
        load.start()
    column = lax.broadcasted_iota(jnp.int32, (16, C), 0)
    blank = jnp.zeros((8, C), F32)
    stores = []
    for which in range(2):
        loads[which].wait()
        for level in range(LEVELS):
            for tile in range(TILES):
                pair = hc_ref[which, level, tile].astype(F32)
                for half in range(2):
                    halo = jnp.concatenate([pair[8 * half : 8 * half + 8], blank], 0)
                    row = 2 * tile + half if tile < 11 else 2 * (tile - 11) + half
                    if tile < 11 and row < ROWS - HALF_ROWS:
                        own = edge[which, level, row].astype(F32)
                        edge[which, level, row] = jnp.where(column < HALF_COLS, halo, own).astype(BF)
                    elif tile >= 11 and row < HALF_ROWS:
                        own = hr_ref[which, level, row, :16].astype(F32)
                        top[which, level, row, :16] = jnp.where(column < HALF_COLS, halo, own).astype(BF)
                        top[which, level, row, 16:] = hr_ref[which, level, row, 16:]
        stores.append(pltpu.make_async_copy(edge.at[which], outs[which].at[:, HALF_ROWS:, :16], sems.at[which]))
        stores.append(pltpu.make_async_copy(top.at[which], outs[which].at[:, :HALF_ROWS], sems.at[2 + which]))
        for store in stores[-2:]:
            store.start()
    for store in stores:
        store.wait()


def merge(out, grad, row_strip, col_strip):
    anywhere = pl.BlockSpec(memory_space=pl.ANY)
    whole = pl.BlockSpec(memory_space=pltpu.VMEM)
    grid_shape = jax.ShapeDtypeStruct((LEVELS, ROWS, COLS, C), BF)
    return pl.pallas_call(
        merge_kernel,
        out_shape=(grid_shape, grid_shape),
        in_specs=[anywhere, anywhere, whole, whole],
        out_specs=(anywhere, anywhere),
        scratch_shapes=[
            pltpu.VMEM((2, LEVELS, ROWS - HALF_ROWS, 16, C), BF),
            pltpu.VMEM((2, LEVELS, HALF_ROWS, COLS, C), BF),
            pltpu.SemaphoreType.DMA((4,)),
        ],
        input_output_aliases={0: 0, 1: 1},
        compiler_params=pltpu.CompilerParams(vmem_limit_bytes=32 * 2**20),
        name="merge",
    )(out, grad, row_strip, col_strip)


def body(latent, cotangent, qkv_weight, out_weight):
    pieces = jnp.concatenate([qkv_weight, out_weight], 1)
    shard = pieces.reshape(4, 2, 4, 256).transpose(1, 0, 2, 3).reshape(2, 16, 256)
    row_strip, col_strip, weights = gather(latent, cotangent, shard)
    out, grad, rows_back, cols_back, dw = layer(
        latent, cotangent, row_strip, col_strip, weights.reshape(C, 4 * C))
    total_tokens = TOKENS * lax.axis_size("lat") * lax.axis_size("lon")
    rows_in, cols_in, sums = reduce(
        rows_back, cols_back, dw.reshape(2, 4, 4, 16, 4 * C), 1.0 / math.sqrt(total_tokens))
    out, grad = merge(out, grad, rows_in, cols_in)
    return out, grad, sums[:, : 3 * C], sums[:, 3 * C :]


def solution(mesh):
    grid = P(None, "lat", "lon", None)
    rows = P(("lat", "lon"), None)
    specs = (grid, grid, rows, rows)
    return jax.shard_map(body, mesh=mesh, in_specs=specs, out_specs=specs, check_vma=False)
```

```python
import functools
import math

import jax
import jax.numpy as jnp
from jax import lax
from jax.experimental import pallas as pl
from jax.experimental.pallas import tpu as pltpu
from jax.sharding import PartitionSpec as P

C = 512
HD = 64
WIN_LAT = 6
WIN_LON = 12
LEVELS = 2
PIECES = LEVELS * WIN_LAT
TOK = PIECES * WIN_LON
SLABS = 4
ACROSS = 4
WINDOWS = SLABS * ACROSS
TOKENS = WINDOWS * TOK
SLAB = ACROSS * TOK
HALF_ROWS = 3
HALF_COLS = 6
ROWS = 24
COLS = 48
TILES = ROWS // 2
HALF = 2 * C
BF = jnp.bfloat16
F32 = jnp.float32


def nn(a, b):
    return lax.dot_general(a, b, (((1,), (0,)), ((), ())), preferred_element_type=F32)


def nt(a, b):
    return lax.dot_general(a, b, (((1,), (1,)), ((), ())), preferred_element_type=F32)


def tn(a, b):
    return lax.dot_general(a, b, (((0,), (0,)), ((), ())), preferred_element_type=F32)


MESH = pl.DeviceIdType.MESH
GROUP = [(a, b, c) for a in range(2) for b in range(2) for c in range(2)][1:]


class Place:
    def __init__(self):
        self.lat, self.lon = lax.axis_index("lat"), lax.axis_index("lon")
        self.x_hi, self.y = self.lat // 4, self.lat % 4
        self.z, self.x_lo, self.core = self.lon // 4, (self.lon // 2) % 2, self.lon % 2

    def mate(self, flips):
        a, b, c = (v + f - 2 * v * f for v, f in zip((self.x_hi, self.x_lo, self.core), flips))
        return (a * 4 + self.y, self.z * 4 + b * 2 + c)

    def along(self, axis, step):
        if axis == "y":
            return (self.x_hi * 4 + (self.y + step) % 4, self.lon)
        return (self.lat, (self.z + step) % 4 * 4 + self.lon % 4)

    def shifted(self, rows, cols):
        return ((self.lat + rows + 8) % 8, (self.lon + cols + 16) % 16)


def greet(senders):
    barrier = pltpu.get_barrier_semaphore()
    for device in senders:
        pl.semaphore_signal(barrier, inc=1, device_id=device, device_id_type=MESH)
    pl.semaphore_wait(barrier, len(senders))


def remote(src, dst, sems, slot, device):
    return pltpu.make_async_remote_copy(
        src_ref=src, dst_ref=dst, send_sem=sems.at[0, slot], recv_sem=sems.at[1, slot],
        device_id=device, device_id_type=MESH)


def partners(place):
    return ([place.mate(f) for f in GROUP]
            + [place.along("y", s) for s in (1, 2, 3)] + [place.along("z", s) for s in (1, 2, 3)])


def fused_kernel(
    factor,
    lat_ref, cot_ref, shard_ref,
    out_ref, grad_ref, back_rows, back_cols, back_corner, sum_qkv, sum_out,
    grid, cols_in, corner_in, strip, corner_strip,
    shard_in, loose, weights,
    rows, window, wide, x_w, inv_w, normed, ctx, gctx, qkv,
    lhs, lhs_t, gp, bias, bias_tail,
    outgoing, rows_out, cols_out, corner_out,
    terms, from_mate, total, sent, from_near, from_far, relay, total2, sent2, from_second, sent3, from_group,
    grid_sems, halo_sems, group_sems, axis_sems, mate_sems, out_sems, back_sems, sum_sems, final_sems,
):
    place = Place()
    loads = [pltpu.make_async_copy(ref, grid.at[i, :, :ROWS], grid_sems.at[i]) for i, ref in enumerate((lat_ref, cot_ref))]
    for load in loads:
        load.start()
    near = [place.shifted(1, 0), place.shifted(0, 1), place.shifted(1, 1),
            place.shifted(-1, 0), place.shifted(0, -1), place.shifted(-1, -1)]
    barrier = pltpu.get_barrier_semaphore()
    for device in partners(place) + near:
        pl.semaphore_signal(barrier, inc=1, device_id=device, device_id_type=MESH)
    down, right, across_down, up, left, across_up = near

    last = lax.axis_index("lat") == lax.axis_size("lat") - 1
    key = lax.broadcasted_iota(jnp.int32, (TOK, 128), 0)
    query = lax.broadcasted_iota(jnp.int32, (TOK, 128), 1)

    def flag(token):
        row = token // WIN_LON
        return jnp.where(row >= WIN_LAT, row - WIN_LAT, row) >= HALF_ROWS

    seam = jnp.where(last, -1e30, 0.0).astype(F32)
    bias[0] = jnp.zeros((TOK, 128), F32)
    bias_tail[0] = jnp.zeros((TOK, 128), F32)
    bias[1] = jnp.where(flag(key) != flag(query), seam, 0.0)
    bias_tail[1] = jnp.where(flag(key), 0.0, seam)

    for which in range(2):
        loads[which].wait()
        for level in range(LEVELS):
            def columns(row):
                return grid[which, level, row, :16].astype(F32)[:8]
            for tile in range(TILES - 1):
                first = HALF_ROWS + 2 * tile
                strip[which, level, tile] = jnp.concatenate(
                    [columns(first), columns(min(first + 1, ROWS - 1))], 0).astype(BF)
            corner_strip[which, level, 0] = jnp.concatenate([columns(0), columns(0)], 0).astype(BF)
            corner_strip[which, level, 1] = jnp.concatenate([columns(1), columns(2)], 0).astype(BF)
    pl.semaphore_wait(barrier, len(partners(place)) + len(near))

    here = (place.x_hi, place.x_lo, place.core)
    group = []
    for slot, flips in enumerate(GROUP):
        copy = remote(shard_ref.at[place.core if flips[2] == 0 else 1 - place.core],
                      shard_in.at[here], group_sems, slot, place.mate(flips))
        copy.start()
        group.append(copy)
    shard_in[here] = shard_ref[place.core]
    halo_cols, halo_rows = [], []
    for which in range(2):
        halo_cols.append(remote(strip.at[which], cols_in.at[which, :, : TILES - 1], halo_sems, which, left))
        halo_rows.append(remote(corner_strip.at[which], corner_in.at[which], halo_sems, 2 + which, across_up))
        for level in range(LEVELS):
            halo_rows.append(remote(grid.at[which, level, :HALF_ROWS], grid.at[which, level, ROWS:], halo_sems,
                                    4 + 2 * which + level, up))
    for copy in halo_cols:
        copy.start()

    for copy in group:
        copy.wait()
    for x_hi in range(2):
        for b in range(2):
            for c in range(2):
                for lane_tile in range(2):
                    line = 16 * (2 * b + c)
                    loose[x_hi, lane_tile, line : line + 16] = (
                        shard_in[x_hi, b, c][:, 128 * lane_tile : 128 * lane_tile + 128].astype(F32))
    for core in range(2):
        half = slice(HALF * core, HALF * (core + 1))

        @pl.when(place.core == core)
        def _():
            for x_hi in range(2):
                for block in range(4):
                    for lane_tile in range(2):
                        start = HALF * core + 256 * block + 128 * lane_tile
                        weights[x_hi, place.y, place.z, :, start : start + 128] = (
                            loose[x_hi, lane_tile, pl.ds(block, 16, stride=4)].astype(BF))
            first, second = ("z", "y") if core == 0 else ("y", "z")
            small = weights.at[:, place.y, place.z, :, half]
            copies = [remote(small, small, axis_sems, step - 1, place.along(first, step)) for step in (1, 2, 3)]
            for copy in copies:
                copy.start()
            for copy in copies:
                copy.wait()
            mine = place.y if core == 0 else place.z

            def block(step, x_hi=slice(None)):
                index = (mine + step) % 4
                return weights.at[x_hi, index, :, :, half] if core == 0 else weights.at[x_hi, :, index, :, half]

            other = place.mate((0, 0, 1))
            ahead = remote(block(0), block(0), axis_sems, 3, place.along(second, 1))
            behind = remote(block(0), block(0), axis_sems, 4, place.along(second, 3))
            ahead.start()
            behind.start()
            mates = [remote(block(0), block(0), mate_sems, 0, other)]
            mates[0].start()
            ahead.wait()
            relays = [remote(block(3, 0), block(3, 0), axis_sems, 5, place.along(second, 1))]
            relays[0].start()
            behind.wait()
            relays.append(remote(block(1, 1), block(1, 1), axis_sems, 6, place.along(second, 3)))
            relays[1].start()
            mates.append(remote(block(3), block(3), mate_sems, 1, other))
            mates.append(remote(block(1), block(1), mate_sems, 2, other))
            mates[1].start()
            mates[2].start()
            for copy in relays:
                copy.wait()
            mates.append(remote(block(2), block(2), mate_sems, 3, other))
            mates[3].start()
            for copy in mates:
                copy.wait()
    for copy in halo_rows:
        copy.start()
    for copy in halo_cols:
        copy.wait()
    w_ref = weights.reshape(C, 4 * C)

    lane = lax.broadcasted_iota(jnp.int32, (1, 128), 1)
    low = (lane < HD).astype(F32).astype(BF)
    high = (lane >= HD).astype(F32).astype(BF)
    low_lanes = lax.broadcasted_iota(jnp.int32, (128, 128), 1) < HD
    low_lanes16 = lax.broadcasted_iota(jnp.int32, (16, 128), 1) < HD

    def spread(tail):
        zero = jnp.zeros((16, 128), BF)
        lines = []
        for head in range(8):
            pair = head // 2
            mine = tail[:, 128 * pair : 128 * (pair + 1)] * (low if head % 2 == 0 else high)
            lines.append(jnp.concatenate([mine if p == pair else zero for p in range(4)], 1))
        return jnp.concatenate(lines, 0)

    def gather(full, pair):
        cols = slice(128 * pair, 128 * (pair + 1))
        return jnp.where(low_lanes16, full[32 * pair : 32 * pair + 16, cols], full[32 * pair + 16 : 32 * pair + 32, cols])

    def softmax_both(scores, grad_att):
        top = jnp.max(scores, 0, keepdims=True)
        raised = jnp.exp(scores - top)
        att = raised * (1.0 / jnp.sum(raised, 0, keepdims=True))
        weighed = grad_att * att
        inner = jnp.sum(weighed, 0, keepdims=True)
        return att.astype(BF), (weighed - att * inner).astype(BF)

    def load_slab(slab, base):
        for which in range(2):
            for level in range(LEVELS):
                for row in range(WIN_LAT):
                    piece = level * WIN_LAT + row
                    rows[which, piece, :COLS] = grid[which, level, slab * WIN_LAT + row + HALF_ROWS].astype(F32)
                    half = row % 2
                    rows[which, piece, COLS:] = (
                        cols_in[which, level, 3 * slab + row // 2].astype(F32)[8 * half : 8 * half + 8])
        for across in range(ACROSS):
            start = HALF_COLS + WIN_LON * across
            part = slice(across * TOK, (across + 1) * TOK)
            for which in range(2):
                for piece in range(PIECES):
                    window[which, WIN_LON * piece : WIN_LON * (piece + 1)] = rows[which, piece, start : start + WIN_LON]
            widened = window[0]
            centred = widened - jnp.mean(widened, -1, keepdims=True)
            inv = lax.rsqrt(jnp.mean(centred * centred, -1, keepdims=True) + 1e-05)
            x_w[part] = widened.astype(BF)
            inv_w[part] = inv
            normed[part] = (centred * inv).astype(BF)
            gp[pl.ds(pl.multiple_of(base + across * TOK, 16), TOK), 3 * C :] = window[1].astype(BF)

    def attend(base, seam_slab):
        offset = bias[seam_slab]
        offset = jnp.concatenate([offset, offset], 1)
        units = []
        for across in range(ACROSS):
            token = across * TOK
            main, tail, whole = slice(token, token + 128), slice(token + 128, token + TOK), slice(token, token + TOK)
            keys = qkv[whole, C : 2 * C]
            values = qkv[whole, 2 * C :]
            units.append((across, None, spread(qkv[tail, :C]), spread(gctx[tail]), keys, values))
            for pair in range(4):
                cols = slice(128 * pair, 128 * (pair + 1))
                q = qkv[main, cols]
                g = gctx[main, cols]
                q_both = jnp.concatenate([q * low, q * high], 0)
                g_both = jnp.concatenate([g * low, g * high], 0)
                units.append((across, pair, q_both, g_both, keys[:, cols], values[:, cols]))
        products = [(nt(k, q), nt(v, g)) for _, _, q, g, k, v in units]
        softened = []
        for unit, (scores, grad_att) in zip(units, products):
            softened.append(softmax_both(scores + (bias_tail[seam_slab] if unit[1] is None else offset), grad_att))
        made = [(tn(a, v), tn(s, k)) for (a, s), (_, _, q, g, k, v) in zip(softened, units)]
        made2 = [(nn(s, q), nn(a, g)) for (a, s), (_, _, q, g, k, v) in zip(softened, units)]
        for unit, (context, grad_q), (grad_k, grad_v) in zip(units, made, made2):
            across, pair = unit[:2]
            if pair is None:
                ctx_tail, gq_tail, gk_tail, gv_tail = context, grad_q, grad_k, grad_v
                continue
            token = across * TOK
            cols = slice(128 * pair, 128 * (pair + 1))
            g_main = pl.ds(pl.multiple_of(base + token, 16), 128)
            g_tail = pl.ds(pl.multiple_of(base + token + 128, 16), 16)
            g_whole = pl.ds(pl.multiple_of(base + token, 16), TOK)
            ctx[token : token + 128, cols] = jnp.where(low_lanes, context[:128], context[128:]).astype(BF)
            ctx[token + 128 : token + TOK, cols] = gather(ctx_tail, pair).astype(BF)
            gp[g_main, cols] = (jnp.where(low_lanes, grad_q[:128], grad_q[128:]) * HD ** -0.5).astype(BF)
            gp[g_tail, cols] = (gather(gq_tail, pair) * HD ** -0.5).astype(BF)
            gp[g_whole, C + 128 * pair : C + 128 * (pair + 1)] = (grad_k + gk_tail[:, cols]).astype(BF)
            gp[g_whole, 2 * C + 128 * pair : 2 * C + 128 * (pair + 1)] = (grad_v + gv_tail[:, cols]).astype(BF)

    def store_slab(slab):
        for which in range(2):
            for level in range(LEVELS):
                for row in range(WIN_LAT):
                    piece = level * WIN_LAT + row
                    for across in range(ACROSS):
                        start = HALF_COLS + WIN_LON * across
                        token = across * TOK + piece * WIN_LON
                        rows[which, piece, start : start + WIN_LON] = wide[which, token : token + WIN_LON]
                    outgoing[slab, which, level, row] = rows[which, piece, :COLS].astype(BF)
                for tile in range(3):
                    piece = level * WIN_LAT + 2 * tile
                    cols_out[which, level, 3 * slab + tile] = jnp.concatenate(
                        [rows[which, piece, COLS:], rows[which, piece + 1, COLS:]], 0).astype(BF)

    def out_copies(slab):
        first = slab * WIN_LAT + HALF_ROWS
        return [pltpu.make_async_copy(outgoing.at[slab, which], target.at[:, pl.ds(first, WIN_LAT)], out_sems.at[slab, which])
                for which, target in enumerate((out_ref, grad_ref))]

    def out_copies_last():
        return [pltpu.make_async_copy(outgoing.at[SLABS - 1, which, :, :HALF_ROWS], target.at[:, ROWS - HALF_ROWS :],
                                      out_sems.at[SLABS - 1, which])
                for which, target in enumerate((out_ref, grad_ref))]

    def back_copies(slab):
        return [remote(cols_out.at[which, :, pl.ds(3 * slab, 3)], back_cols.at[which, :, pl.ds(3 * slab, 3)], back_sems,
                       2 * slab + which, right) for which in range(2)]

    def back_copies_last():
        copies = []
        for which in range(2):
            copies.append(remote(outgoing.at[SLABS - 1, which, :, HALF_ROWS:], back_rows.at[which], back_sems, 8 + which, down))
            copies.append(remote(cols_out.at[which, :, TILES - 2 :], back_corner.at[which], back_sems, 10 + which, across_down))
        return copies

    @pl.loop(0, SLABS)
    def _(step):
        slab = step + (step // 2) * (1 - 2 * (step % 2))
        base = pl.multiple_of(step * SLAB, 64)

        @pl.when(step == 2)
        def _():
            for copy in halo_rows:
                copy.wait()
            for which in range(2):
                for level in range(LEVELS):
                    cols_in[which, level, TILES - 2] = jnp.concatenate(
                        [cols_in[which, level, TILES - 2].astype(F32)[:8], corner_in[which, level, 0].astype(F32)[8:]], 0).astype(BF)
                    cols_in[which, level, TILES - 1] = corner_in[which, level, 1]

        load_slab(slab, base)
        block = normed[...]
        lhs[0, pl.ds(pl.multiple_of((step % 2) * SLAB, 64), SLAB)] = block
        for third in range(3):
            cols = slice(C * third, C * (third + 1))
            projected = nn(block, w_ref[:, cols]).astype(BF)
            qkv[:, cols] = projected * BF(HD ** -0.5) if third == 0 else projected
        gctx[...] = nt(gp[pl.ds(base, SLAB), 3 * C :], w_ref[:, 3 * C :]).astype(BF)
        attend(base, step // 2 * (1 - step % 2))
        context = ctx[...]
        lhs[1, pl.ds(pl.multiple_of((step % 2) * SLAB, 64), SLAB)] = context
        wide[0] = x_w[...].astype(F32) + nn(context, w_ref[:, 3 * C :])
        grad_normed = nt(gp[pl.ds(base, SLAB), : 3 * C], w_ref[:, : 3 * C])
        standard = normed[...].astype(F32)
        first_mean = jnp.mean(grad_normed, -1, keepdims=True)
        second_mean = jnp.mean(grad_normed * standard, -1, keepdims=True)
        wide[1] = inv_w[...] * (grad_normed - first_mean - standard * second_mean) + gp[pl.ds(base, SLAB), 3 * C :].astype(F32)
        store_slab(slab)
        for copy in back_copies(slab):
            copy.start()

        @pl.when(step == 2)
        def _():
            for copy in out_copies_last() + back_copies_last():
                copy.start()

        @pl.when(step != 2)
        def _():
            for copy in out_copies(slab):
                copy.start()

        @pl.when(step % 2 == 1)
        def _():
            for which in range(2):
                lhs_t[which, :, pl.ds(pl.multiple_of(step // 2 * (2 * SLAB), 128), 2 * SLAB)] = lhs[which].T

    other = place.mate((0, 0, 1))

    def columns_of(half, part):
        return (half * 2 + part) % 4

    def product(block):
        return nn(lhs_t[block // 3], gp[:, pl.ds(pl.multiple_of(block * C, 128), C)])

    def mate_copy(part):
        return remote(terms.at[part], from_mate.at[part], sum_sems, part, other)

    @pl.loop(0, 2)
    def _(part):
        terms[part] = product(columns_of(1 - place.core, part)).astype(BF).reshape(2, 4, 4, 16, C)
        mate_copy(part).start()

    @pl.loop(0, 2)
    def _(part):
        mate_copy(part).wait()
        added = product(columns_of(place.core, part)) + from_mate[part].reshape(C, C).astype(F32)
        total[part] = added.reshape(2, 4, 4, 16, C)
        sent[part] = added.astype(BF).reshape(2, 4, 4, 16, C)

    for core in range(2):
        @pl.when(place.core == core)
        def _():
            first, second = ("y", "z") if core == 0 else ("z", "y")
            mine = place.y if core == 0 else place.z

            def block(ref, step, x_hi):
                index = (mine + step) % 4
                return ref.at[:, x_hi, index] if core == 0 else ref.at[:, x_hi, :, index]

            ahead, behind = place.along(first, 1), place.along(first, 3)
            far = [remote(block(sent, 2, 0), from_far.at[0], sum_sems, 2, ahead),
                   remote(block(sent, 2, 1), from_far.at[1], sum_sems, 3, behind)]
            plain = [remote(block(sent, 1, 1), from_near.at[0, 1], sum_sems, 4, ahead),
                     remote(block(sent, 3, 0), from_near.at[1, 0], sum_sems, 5, behind)]
            for copy in far + plain:
                copy.start()
            summed = []
            for way, (step, x_hi, device) in enumerate(((1, 0, ahead), (3, 1, behind))):
                far[way].wait()
                relay[way] = (block(total, step, x_hi)[...] + from_far[way].astype(F32)).astype(BF)
                summed.append(remote(relay.at[way], from_near.at[way, x_hi], sum_sems, 6 + way, device))
                summed[way].start()
            for copy in plain + summed:
                copy.wait()
            for x_hi in range(2):
                added = block(total, 0, x_hi)[...] + from_near[0, x_hi].astype(F32) + from_near[1, x_hi].astype(F32)
                total2[x_hi] = added
                sent2[x_hi] = added.astype(BF)
            mine2 = place.z if core == 0 else place.y
            copies = [remote(sent2.at[:, :, (mine2 + step) % 4], from_second.at[step - 1], sum_sems, 8 + step - 1,
                             place.along(second, step)) for step in (1, 2, 3)]
            for copy in copies:
                copy.start()
            for copy in copies:
                copy.wait()
            added = total2[:, :, mine2]
            for step in range(3):
                added = added + from_second[step].astype(F32)
            sent3[...] = added.astype(BF)

    copies = []
    for slot, flips in enumerate(GROUP):
        target = place.x_hi if flips[0] == 0 else 1 - place.x_hi
        copies.append(remote(sent3.at[target], from_group.at[here], final_sems, slot, place.mate(flips)))
    for copy in copies:
        copy.start()
    from_group[here] = sent3[place.x_hi]
    for copy in copies:
        copy.wait()
    position = place.x_lo * 2 + place.core
    for block in range(4):
        added = from_group[0, 0, block // 2, block % 2].astype(F32)
        for a, b in ((0, 1), (1, 0), (1, 1)):
            added = added + from_group[a, b, block // 2, block % 2].astype(F32)
        picked = added[:4]
        for i in range(1, 4):
            picked = jnp.where(position == i, added[4 * i : 4 * i + 4], picked)
        if block < 3:
            sum_qkv[:, C * block : C * (block + 1)] = picked * factor
        else:
            sum_out[...] = picked * factor
    for slab in range(SLABS):
        for copy in back_copies(slab):
            copy.wait()
    for slab in range(SLABS - 1):
        for copy in out_copies(slab):
            copy.wait()
    for copy in out_copies_last() + back_copies_last():
        copy.wait()


def fused(latent, cotangent, shard, factor):
    anywhere = pl.BlockSpec(memory_space=pl.ANY)
    whole = pl.BlockSpec(memory_space=pltpu.VMEM)
    grid_shape = jax.ShapeDtypeStruct((LEVELS, ROWS, COLS, C), BF)
    dma = pltpu.SemaphoreType.DMA
    return pl.pallas_call(
        functools.partial(fused_kernel, factor),
        out_shape=(
            grid_shape,
            grid_shape,
            jax.ShapeDtypeStruct((2, LEVELS, HALF_ROWS, COLS, C), BF),
            jax.ShapeDtypeStruct((2, LEVELS, TILES, 16, C), BF),
            jax.ShapeDtypeStruct((2, LEVELS, 2, 16, C), BF),
            jax.ShapeDtypeStruct((4, 3 * C), F32),
            jax.ShapeDtypeStruct((4, C), F32),
        ),
        in_specs=[anywhere, anywhere, whole],
        out_specs=(anywhere,) * 5 + (whole,) * 2,
        scratch_shapes=[
            pltpu.VMEM((2, LEVELS, ROWS + HALF_ROWS, COLS, C), BF),
            pltpu.VMEM((2, LEVELS, TILES, 16, C), BF),
            pltpu.VMEM((2, LEVELS, 2, 16, C), BF),
            pltpu.VMEM((2, LEVELS, TILES - 1, 16, C), BF),
            pltpu.VMEM((2, LEVELS, 2, 16, C), BF),
            pltpu.VMEM((2, 2, 2, 16, 256), BF),
            pltpu.VMEM((2, 2, 64, 128), F32),
            pltpu.VMEM((2, 4, 4, 16, 4 * C), BF),
            pltpu.VMEM((2, PIECES, COLS + 8, C), F32),
            pltpu.VMEM((2, TOK, C), F32),
            pltpu.VMEM((2, SLAB, C), F32),
            pltpu.VMEM((SLAB, C), BF),
            pltpu.VMEM((SLAB, 1), F32),
            pltpu.VMEM((SLAB, C), BF),
            pltpu.VMEM((SLAB, C), BF),
            pltpu.VMEM((SLAB, C), BF),
            pltpu.VMEM((SLAB, 3 * C), BF),
            pltpu.VMEM((2, 2 * SLAB, C), BF),
            pltpu.VMEM((2, C, TOKENS), BF),
            pltpu.VMEM((TOKENS, 4 * C), BF),
            pltpu.VMEM((2, TOK, 128), F32),
            pltpu.VMEM((2, TOK, 128), F32),
            pltpu.VMEM((SLABS, 2, LEVELS, WIN_LAT, COLS, C), BF),
            pltpu.VMEM((8, 128), F32),
            pltpu.VMEM((2, LEVELS, TILES, 16, C), BF),
            pltpu.VMEM((8, 128), F32),
            pltpu.VMEM((2, 2, 4, 4, 16, C), BF),
            pltpu.VMEM((2, 2, 4, 4, 16, C), BF),
            pltpu.VMEM((2, 2, 4, 4, 16, C), F32),
            pltpu.VMEM((2, 2, 4, 4, 16, C), BF),
            pltpu.VMEM((2, 2, 2, 4, 16, C), BF),
            pltpu.VMEM((2, 2, 4, 16, C), BF),
            pltpu.VMEM((2, 2, 4, 16, C), BF),
            pltpu.VMEM((2, 2, 4, 16, C), F32),
            pltpu.VMEM((2, 2, 4, 16, C), BF),
            pltpu.VMEM((3, 2, 2, 16, C), BF),
            pltpu.VMEM((2, 2, 16, C), BF),
            pltpu.VMEM((2, 2, 2, 2, 16, C), BF),
            dma((2,)),
            dma((2, 8)),
            dma((2, 7)),
            dma((2, 7)),
            dma((2, 4)),
            dma((SLABS, 2)),
            dma((2, 12)),
            dma((2, 11)),
            dma((2, 7)),
        ],
        compiler_params=pltpu.CompilerParams(
            collective_id=0, has_side_effects=True, vmem_limit_bytes=62 * 2**20),
        name="layer",
    )(latent, cotangent, shard)


def merge_kernel(out_in, grad_in, hr_ref, hc_ref, hd_ref, out_ref, grad_ref, edge, top, sems):
    del out_in, grad_in
    outs = (out_ref, grad_ref)
    loads = [pltpu.make_async_copy(ref.at[:, HALF_ROWS:, :16], edge.at[i], sems.at[i]) for i, ref in enumerate(outs)]
    for load in loads:
        load.start()
    column = lax.broadcasted_iota(jnp.int32, (16, C), 0)
    blank = jnp.zeros((8, C), F32)
    stores = []
    for which in range(2):
        loads[which].wait()
        for level in range(LEVELS):
            for row in range(ROWS):
                line = (row - HALF_ROWS) % ROWS
                ref = hc_ref if row >= HALF_ROWS else hd_ref
                tile = line // 2 if row >= HALF_ROWS else line // 2 - (TILES - 2)
                half = line % 2
                halo = jnp.concatenate([ref[which, level, tile].astype(F32)[8 * half : 8 * half + 8], blank], 0)
                if row >= HALF_ROWS:
                    own = edge[which, level, row - HALF_ROWS].astype(F32)
                    edge[which, level, row - HALF_ROWS] = jnp.where(column < HALF_COLS, halo, own).astype(BF)
                else:
                    own = hr_ref[which, level, row, :16].astype(F32)
                    top[which, level, row, :16] = jnp.where(column < HALF_COLS, halo, own).astype(BF)
                    top[which, level, row, 16:] = hr_ref[which, level, row, 16:]
        stores.append(pltpu.make_async_copy(edge.at[which], outs[which].at[:, HALF_ROWS:, :16], sems.at[which]))
        stores.append(pltpu.make_async_copy(top.at[which], outs[which].at[:, :HALF_ROWS], sems.at[2 + which]))
        for store in stores[-2:]:
            store.start()
    for store in stores:
        store.wait()


def merge(out, grad, row_strip, col_strip, corner):
    anywhere = pl.BlockSpec(memory_space=pl.ANY)
    whole = pl.BlockSpec(memory_space=pltpu.VMEM)
    grid_shape = jax.ShapeDtypeStruct((LEVELS, ROWS, COLS, C), BF)
    return pl.pallas_call(
        merge_kernel,
        out_shape=(grid_shape, grid_shape),
        in_specs=[anywhere, anywhere, whole, whole, whole],
        out_specs=(anywhere, anywhere),
        scratch_shapes=[
            pltpu.VMEM((2, LEVELS, ROWS - HALF_ROWS, 16, C), BF),
            pltpu.VMEM((2, LEVELS, HALF_ROWS, COLS, C), BF),
            pltpu.SemaphoreType.DMA((4,)),
        ],
        input_output_aliases={0: 0, 1: 1},
        compiler_params=pltpu.CompilerParams(vmem_limit_bytes=32 * 2**20),
        name="merge",
    )(out, grad, row_strip, col_strip, corner)


def body(latent, cotangent, qkv_weight, out_weight):
    pieces = jnp.concatenate([qkv_weight, out_weight], 1)
    shard = pieces.reshape(4, 2, 4, 256).transpose(1, 0, 2, 3).reshape(2, 16, 256)
    total_tokens = TOKENS * lax.axis_size("lat") * lax.axis_size("lon")
    out, grad, rows_in, cols_in, corner, sum_qkv, sum_out = fused(
        latent, cotangent, shard, 1.0 / math.sqrt(total_tokens))
    out, grad = merge(out, grad, rows_in, cols_in, corner)
    return out, grad, sum_qkv, sum_out


def solution(mesh):
    grid = P(None, "lat", "lon", None)
    rows = P(("lat", "lon"), None)
    specs = (grid, grid, rows, rows)
    return jax.shard_map(body, mesh=mesh, in_specs=specs, out_specs=specs, check_vma=False)
```

```python
import functools
import math

import jax
import jax.numpy as jnp
from jax import lax
from jax.experimental import pallas as pl
from jax.experimental.pallas import tpu as pltpu
from jax.sharding import PartitionSpec as P

C = 512
HD = 64
WIN_LAT = 6
WIN_LON = 12
LEVELS = 2
PIECES = LEVELS * WIN_LAT
TOK = PIECES * WIN_LON
SLABS = 4
ACROSS = 4
WINDOWS = SLABS * ACROSS
TOKENS = WINDOWS * TOK
SLAB = ACROSS * TOK
HALF_ROWS = 3
HALF_COLS = 6
ROWS = 24
COLS = 48
TILES = ROWS // 2
HALF = 2 * C
BF = jnp.bfloat16
F32 = jnp.float32


def nn(a, b):
    return lax.dot_general(a, b, (((1,), (0,)), ((), ())), preferred_element_type=F32)


def nt(a, b):
    return lax.dot_general(a, b, (((1,), (1,)), ((), ())), preferred_element_type=F32)


def tn(a, b):
    return lax.dot_general(a, b, (((0,), (0,)), ((), ())), preferred_element_type=F32)


MESH = pl.DeviceIdType.MESH
GROUP = [(a, b, c) for a in range(2) for b in range(2) for c in range(2)][1:]


EDGE_STEP, ROWS_STEP = 2, 3


def first_token(slab, across):
    if isinstance(slab, int) and slab == SLABS - 1:
        return SLAB * ROWS_STEP + TOK * across
    if across == ACROSS - 1:
        return pl.multiple_of(SLAB * EDGE_STEP + TOK * (slab + 1), 16)
    return pl.multiple_of(TOK * (3 * slab + across), 16)


class Place:
    def __init__(self):
        self.lat, self.lon = lax.axis_index("lat"), lax.axis_index("lon")
        self.x_hi, self.y = self.lat // 4, self.lat % 4
        self.z, self.x_lo, self.core = self.lon // 4, (self.lon // 2) % 2, self.lon % 2

    def mate(self, flips):
        a, b, c = (v + f - 2 * v * f for v, f in zip((self.x_hi, self.x_lo, self.core), flips))
        return (a * 4 + self.y, self.z * 4 + b * 2 + c)

    def along(self, axis, step):
        if axis == "y":
            return (self.x_hi * 4 + (self.y + step) % 4, self.lon)
        return (self.lat, (self.z + step) % 4 * 4 + self.lon % 4)

    def shifted(self, rows, cols):
        return ((self.lat + rows + 8) % 8, (self.lon + cols + 16) % 16)


def greet(senders):
    barrier = pltpu.get_barrier_semaphore()
    for device in senders:
        pl.semaphore_signal(barrier, inc=1, device_id=device, device_id_type=MESH)
    pl.semaphore_wait(barrier, len(senders))


def remote(src, dst, sems, slot, device):
    return pltpu.make_async_remote_copy(
        src_ref=src, dst_ref=dst, send_sem=sems.at[0, slot], recv_sem=sems.at[1, slot],
        device_id=device, device_id_type=MESH)


def partners(place):
    return ([place.mate(f) for f in GROUP]
            + [place.along("y", s) for s in (1, 2, 3)] + [place.along("z", s) for s in (1, 2, 3)])


def fused_kernel(
    factor,
    lat_ref, cot_ref, qkv_shard, out_shard,
    out_ref, grad_ref, back_rows, back_cols, back_corner, sums_ref,
    grid, cols_in, corner_in, strip, corner_strip,
    shard_ref, shard_in, loose, weights,
    rows, window, results, inv_w, normed, ctx, gctx, qkv,
    lhs_t, gp, bias, bias_tail,
    cols_out,
    terms, from_mate, total, sent, from_near, from_far, relay, total2, sent2, from_second, sent3, from_group,
    grid_sems, halo_sems, group_sems, axis_sems, mate_sems, out_sems, back_sems, sum_sems, final_sems,
):
    place = Place()
    loads = [pltpu.make_async_copy(ref, grid.at[i, :, :ROWS], grid_sems.at[i]) for i, ref in enumerate((lat_ref, cot_ref))]
    for load in loads:
        load.start()
    near = [place.shifted(1, 0), place.shifted(0, 1), place.shifted(1, 1),
            place.shifted(-1, 0), place.shifted(0, -1), place.shifted(-1, -1)]
    barrier = pltpu.get_barrier_semaphore()
    for device in partners(place) + near:
        pl.semaphore_signal(barrier, inc=1, device_id=device, device_id_type=MESH)
    down, right, across_down, up, left, across_up = near

    def both(stage):
        for core in range(2):
            pl.when(place.core == core)(functools.partial(stage, core))

    for core in range(2):
        for block in range(4):
            for lane_tile in range(2):
                start = HALF * core + 256 * block + 128 * lane_tile
                piece = qkv_shard[:, start : start + 128] if start < 3 * C else out_shard[:, start - 3 * C : start - 3 * C + 128]
                loose[core, lane_tile, pl.ds(block, 4, stride=4)] = piece.astype(F32)
        shard_ref[core] = jnp.concatenate([loose[core, 0, :16], loose[core, 1, :16]], 1).astype(BF)

    pl.semaphore_wait(barrier, len(partners(place)) + len(near))

    here = (place.x_hi, place.x_lo, place.core)
    group = []
    for slot, flips in enumerate(GROUP):
        copy = remote(shard_ref.at[place.core if flips[2] == 0 else 1 - place.core],
                      shard_in.at[here], group_sems, slot, place.mate(flips))
        copy.start()
        group.append(copy)
    shard_in[here] = shard_ref[place.core]

    last = lax.axis_index("lat") == lax.axis_size("lat") - 1
    key = lax.broadcasted_iota(jnp.int32, (TOK, 128), 0)
    query = lax.broadcasted_iota(jnp.int32, (TOK, 128), 1)

    def flag(token):
        row = token // WIN_LON
        return jnp.where(row >= WIN_LAT, row - WIN_LAT, row) >= HALF_ROWS

    seam = jnp.where(last, -1e30, 0.0).astype(F32)
    bias[0] = jnp.zeros((TOK, 128), F32)
    bias_tail[0] = jnp.zeros((TOK, 128), F32)
    bias[1] = jnp.where(flag(key) != flag(query), seam, 0.0)
    bias_tail[1] = jnp.where(flag(key), 0.0, seam)

    for which in range(2):
        loads[which].wait()
        for level in range(LEVELS):
            def columns(row):
                return grid[which, level, row, :16].astype(F32)[:8]
            for tile in range(TILES - 1):
                first = HALF_ROWS + 2 * tile
                strip[which, level, tile] = jnp.concatenate(
                    [columns(first), columns(min(first + 1, ROWS - 1))], 0).astype(BF)
            corner_strip[which, level, 0] = jnp.concatenate([columns(0), columns(0)], 0).astype(BF)
            corner_strip[which, level, 1] = jnp.concatenate([columns(1), columns(2)], 0).astype(BF)
    halo_cols, halo_rows = [], []
    for which in range(2):
        halo_cols.append(remote(strip.at[which], cols_in.at[which, :, : TILES - 1], halo_sems, which, left))
        halo_rows.append(remote(corner_strip.at[which], corner_in.at[which], halo_sems, 2 + which, across_up))
        for level in range(LEVELS):
            halo_rows.append(remote(grid.at[which, level, :HALF_ROWS], grid.at[which, level, ROWS:], halo_sems,
                                    4 + 2 * which + level, up))

    for copy in group:
        copy.wait()
    for x_hi in range(2):
        for b in range(2):
            for c in range(2):
                for lane_tile in range(2):
                    line = 16 * (2 * b + c)
                    loose[x_hi, lane_tile, line : line + 16] = (
                        shard_in[x_hi, b, c][:, 128 * lane_tile : 128 * lane_tile + 128].astype(F32))
    def load_window(slab, across):
        start = HALF_COLS + WIN_LON * across
        low_col, high_col = start // 16 * 16, min(-(-(start + WIN_LON) // 16) * 16, COLS)
        for which in range(2):
            for level in range(LEVELS):
                for row in range(WIN_LAT):
                    piece = level * WIN_LAT + row
                    rows[which, piece, low_col:high_col] = (
                        grid[which, level, slab * WIN_LAT + row + HALF_ROWS, low_col:high_col].astype(F32))
                    if across == ACROSS - 1:
                        half = row % 2
                        rows[which, piece, COLS:] = (
                            cols_in[which, level, 3 * slab + row // 2].astype(F32)[8 * half : 8 * half + 8])
                    window[which, WIN_LON * piece : WIN_LON * (piece + 1)] = rows[which, piece, start : start + WIN_LON]
        part = pl.ds(first_token(slab, across), TOK)
        widened = window[0]
        centred = widened - jnp.mean(widened, -1, keepdims=True)
        inv = lax.rsqrt(jnp.mean(centred * centred, -1, keepdims=True) + 1e-05)
        results[0, part] = widened.astype(BF)
        inv_w[part] = inv
        normed[part] = (centred * inv).astype(BF)
        gp[part, 3 * C :] = window[1].astype(BF)

    def small_copies(core):
        block = weights.at[:, place.y, place.z, :, HALF * core : HALF * (core + 1)]
        return [remote(block, block, axis_sems, step - 1, place.along("z" if core == 0 else "y", step)) for step in (1, 2, 3)]

    def ring_block(core, step, x_hi=slice(None)):
        half = slice(HALF * core, HALF * (core + 1))
        if core == 0:
            return weights.at[x_hi, (place.y + step) % 4, :, :, half]
        return weights.at[x_hi, :, (place.z + step) % 4, :, half]

    def ring_copies(core):
        axis = "y" if core == 0 else "z"
        ahead, behind = place.along(axis, 1), place.along(axis, 3)
        piece = [ring_block(core, 0, 0), ring_block(core, 0, 1)]
        far, near = ring_block(core, 3, 0), ring_block(core, 1, 1)
        return ([remote(piece[i], piece[i], axis_sems, 3 + i, ahead) for i in (0, 1)],
                [remote(piece[i], piece[i], axis_sems, 5 + i, behind) for i in (1, 0)],
                [remote(far, far, axis_sems, 7, ahead), remote(near, near, axis_sems, 8, behind)])

    def mate_copies(core):
        other = place.mate((0, 0, 1))
        return [remote(ring_block(core, step), ring_block(core, step), mate_sems, slot, other)
                for slot, step in enumerate((0, 3, 1, 2))]

    def spread_shards(core):
        for x_hi in range(2):
            for block in range(4):
                for lane_tile in range(2):
                    start = HALF * core + 256 * block + 128 * lane_tile
                    weights[x_hi, place.y, place.z, :, start : start + 128] = (
                        loose[x_hi, lane_tile, pl.ds(block, 16, stride=4)].astype(BF))
        for copy in small_copies(core):
            copy.start()

    def ring_start(core):
        for copy in small_copies(core):
            copy.wait()
        ahead, behind, _ = ring_copies(core)
        for one, other in zip(ahead, behind):
            one.start()
            other.start()
        mate_copies(core)[0].start()

    def ring_relay(core):
        ahead, behind, far = ring_copies(core)
        mates = mate_copies(core)
        ahead[0].wait()
        far[0].start()
        behind[0].wait()
        far[1].start()
        ahead[1].wait()
        behind[1].wait()
        mates[1].start()
        mates[2].start()

    def ring_end(core):
        for copy in ring_copies(core)[2]:
            copy.wait()
        mate_copies(core)[3].start()

    def mates_end(core):
        for copy in mate_copies(core):
            copy.wait()

    @pl.loop(0, SLABS - 1)
    def _(slab):
        for when, stage in enumerate((spread_shards, ring_start, ring_relay)):
            for core in range(2):
                pl.when((slab == when) & (place.core == core))(functools.partial(stage, core))
        for across in range(ACROSS - 1):
            load_window(slab, across)

    both(ring_end)
    for copy in halo_cols + halo_rows:
        copy.start()
    both(mates_end)
    w_ref = weights.reshape(C, 4 * C)

    lane = lax.broadcasted_iota(jnp.int32, (1, 128), 1)
    low = (lane < HD).astype(F32).astype(BF)
    high = (lane >= HD).astype(F32).astype(BF)
    low_lanes = lax.broadcasted_iota(jnp.int32, (128, 128), 1) < HD
    low_lanes16 = lax.broadcasted_iota(jnp.int32, (16, 128), 1) < HD

    def spread(tail):
        zero = jnp.zeros((16, 128), BF)
        lines = []
        for head in range(8):
            pair = head // 2
            mine = tail[:, 128 * pair : 128 * (pair + 1)] * (low if head % 2 == 0 else high)
            lines.append(jnp.concatenate([mine if p == pair else zero for p in range(4)], 1))
        return jnp.concatenate(lines, 0)

    def gather(full, pair):
        cols = slice(128 * pair, 128 * (pair + 1))
        return jnp.where(low_lanes16, full[32 * pair : 32 * pair + 16, cols], full[32 * pair + 16 : 32 * pair + 32, cols])

    def softmax_both(scores, grad_att):
        top = jnp.max(scores, 0, keepdims=True)
        raised = jnp.exp(scores - top)
        att = raised * (1.0 / jnp.sum(raised, 0, keepdims=True))
        weighed = grad_att * att
        inner = jnp.sum(weighed, 0, keepdims=True)
        return att.astype(BF), (weighed - att * inner).astype(BF)

    def attend(base, seam_slab):
        offset = bias[seam_slab]
        offset = jnp.concatenate([offset, offset], 1)
        units = []
        for across in range(ACROSS):
            token = across * TOK
            main, tail, whole = slice(token, token + 128), slice(token + 128, token + TOK), slice(token, token + TOK)
            keys = qkv[whole, C : 2 * C]
            values = qkv[whole, 2 * C :]
            units.append((across, None, spread(qkv[tail, :C]), spread(gctx[tail]), keys, values))
            for pair in range(4):
                cols = slice(128 * pair, 128 * (pair + 1))
                q = qkv[main, cols]
                g = gctx[main, cols]
                q_both = jnp.concatenate([q * low, q * high], 0)
                g_both = jnp.concatenate([g * low, g * high], 0)
                units.append((across, pair, q_both, g_both, keys[:, cols], values[:, cols]))
        products = [(nt(k, q), nt(v, g)) for _, _, q, g, k, v in units]
        softened = []
        for unit, (scores, grad_att) in zip(units, products):
            softened.append(softmax_both(scores + (bias_tail[seam_slab] if unit[1] is None else offset), grad_att))
        made = [(tn(a, v), tn(s, k)) for (a, s), (_, _, q, g, k, v) in zip(softened, units)]
        made2 = [(nn(s, q), nn(a, g)) for (a, s), (_, _, q, g, k, v) in zip(softened, units)]
        for unit, (context, grad_q), (grad_k, grad_v) in zip(units, made, made2):
            across, pair = unit[:2]
            if pair is None:
                ctx_tail, gq_tail, gk_tail, gv_tail = context, grad_q, grad_k, grad_v
                continue
            token = across * TOK
            cols = slice(128 * pair, 128 * (pair + 1))
            g_main = pl.ds(pl.multiple_of(base + token, 16), 128)
            g_tail = pl.ds(pl.multiple_of(base + token + 128, 16), 16)
            g_whole = pl.ds(pl.multiple_of(base + token, 16), TOK)
            ctx[g_main, cols] = jnp.where(low_lanes, context[:128], context[128:]).astype(BF)
            ctx[g_tail, cols] = gather(ctx_tail, pair).astype(BF)
            gp[g_main, cols] = (jnp.where(low_lanes, grad_q[:128], grad_q[128:]) * HD ** -0.5).astype(BF)
            gp[g_tail, cols] = (gather(gq_tail, pair) * HD ** -0.5).astype(BF)
            gp[g_whole, C + 128 * pair : C + 128 * (pair + 1)] = (grad_k + gk_tail[:, cols]).astype(BF)
            gp[g_whole, 2 * C + 128 * pair : 2 * C + 128 * (pair + 1)] = (grad_v + gv_tail[:, cols]).astype(BF)

    def results_to_rows(slab, across):
        part = pl.ds(first_token(slab, across), TOK)
        start = HALF_COLS + WIN_LON * across
        for which in range(2):
            window[which] = results[which, part].astype(F32)
            for piece in range(PIECES):
                rows[which, piece, start : start + WIN_LON] = window[which, WIN_LON * piece : WIN_LON * (piece + 1)]

    def rows_to_strip(slab):
        for which in range(2):
            for level in range(LEVELS):
                for tile in range(3):
                    piece = level * WIN_LAT + 2 * tile
                    cols_out[which, level, 3 * slab + tile] = jnp.concatenate(
                        [rows[which, piece, COLS:], rows[which, piece + 1, COLS:]], 0).astype(BF)

    def store_slab(slab):
        for across in range(ACROSS):
            results_to_rows(slab, across)
        for which in range(2):
            for level in range(LEVELS):
                for row in range(WIN_LAT):
                    grid[which, level, slab * WIN_LAT + row + HALF_ROWS] = rows[which, level * WIN_LAT + row, :COLS].astype(BF)

    def out_copies(slab):
        first = slab * WIN_LAT + HALF_ROWS
        return [pltpu.make_async_copy(grid.at[which, :, pl.ds(first, WIN_LAT)], target.at[:, pl.ds(first, WIN_LAT)], out_sems.at[slab, which])
                for which, target in enumerate((out_ref, grad_ref))]

    def out_copies_last():
        return [pltpu.make_async_copy(grid.at[which, :, ROWS - HALF_ROWS : ROWS], target.at[:, ROWS - HALF_ROWS :],
                                      out_sems.at[SLABS - 1, which])
                for which, target in enumerate((out_ref, grad_ref))]

    def back_copies(slab):
        return [remote(cols_out.at[which, :, pl.ds(3 * slab, 3)], back_cols.at[which, :, pl.ds(3 * slab, 3)], back_sems,
                       2 * slab + which, right) for which in range(2)]

    def back_copies_last():
        copies = []
        for which in range(2):
            copies.append(remote(grid.at[which, :, ROWS:], back_rows.at[which], back_sems, 8 + which, down))
            copies.append(remote(cols_out.at[which, :, TILES - 2 :], back_corner.at[which], back_sems, 10 + which, across_down))
        return copies

    def finish(unit):
        part = pl.ds(pl.multiple_of(unit * SLAB, 64), SLAB)
        results[0, part] = (results[0, part].astype(F32) + nn(ctx[part], w_ref[:, 3 * C :])).astype(BF)
        grad_normed = nt(gp[part, : 3 * C], w_ref[:, : 3 * C])
        standard = normed[part].astype(F32)
        first_mean = jnp.mean(grad_normed, -1, keepdims=True)
        second_mean = jnp.mean(grad_normed * standard, -1, keepdims=True)
        results[1, part] = (inv_w[part] * (grad_normed - first_mean - standard * second_mean)
                            + gp[part, 3 * C :].astype(F32)).astype(BF)

    @pl.loop(0, SLABS)
    def _(step):
        base = pl.multiple_of(step * SLAB, 64)
        part = pl.ds(base, SLAB)

        @pl.when(step == 2)
        def _():
            for copy in halo_cols:
                copy.wait()

        @pl.when(step == EDGE_STEP)
        def _():
            @pl.loop(0, SLABS - 1)
            def _(slab):
                load_window(slab, ACROSS - 1)

        @pl.when(step == ROWS_STEP)
        def _():
            for copy in halo_rows:
                copy.wait()
            for which in range(2):
                for level in range(LEVELS):
                    cols_in[which, level, TILES - 2] = jnp.concatenate(
                        [cols_in[which, level, TILES - 2].astype(F32)[:8], corner_in[which, level, 0].astype(F32)[8:]], 0).astype(BF)
                    cols_in[which, level, TILES - 1] = corner_in[which, level, 1]
            for across in range(ACROSS):
                load_window(SLABS - 1, across)

        block = normed[part]
        for third in range(3):
            cols = slice(C * third, C * (third + 1))
            projected = nn(block, w_ref[:, cols]).astype(BF)
            qkv[:, cols] = projected * BF(HD ** -0.5) if third == 0 else projected
        gctx[...] = nt(gp[part, 3 * C :], w_ref[:, 3 * C :]).astype(BF)
        attend(base, step // 3 if ROWS_STEP == 3 else step // 2 * (1 - step // 3))
        @pl.when(step >= 2)
        def _():
            finish(step)

        @pl.when(step == EDGE_STEP)
        def _():
            @pl.loop(0, SLABS - 1)
            def _(slab):
                results_to_rows(slab, ACROSS - 1)
                rows_to_strip(slab)
                for copy in back_copies(slab):
                    copy.start()

        @pl.when(step == ROWS_STEP)
        def _():
            store_slab(SLABS - 1)
            rows_to_strip(SLABS - 1)
            for copy in back_copies_last() + back_copies(SLABS - 1) + out_copies_last():
                copy.start()

        @pl.when(step % 2 == 1)
        def _():
            two = pl.ds(pl.multiple_of(step // 2 * (2 * SLAB), 128), 2 * SLAB)
            lhs_t[0, :, two] = normed[two].T
            lhs_t[1, :, two] = ctx[two].T

    other = place.mate((0, 0, 1))

    def columns_of(half, part):
        return (half * 2 + part) % 4

    def product(block):
        return nn(lhs_t[block // 3], gp[:, pl.ds(pl.multiple_of(block * C, 128), C)])

    def mate_copy(part):
        return remote(terms.at[part], from_mate.at[part], sum_sems, part, other)

    @pl.loop(0, 2)
    def _(part):
        terms[part] = product(columns_of(1 - place.core, part)).astype(BF).reshape(2, 4, 4, 16, C)
        mate_copy(part).start()

    @pl.loop(0, 2)
    def _(part):
        mate_copy(part).wait()
        added = product(columns_of(place.core, part)) + from_mate[part].reshape(C, C).astype(F32)
        total[part] = added.reshape(2, 4, 4, 16, C)
        sent[part] = added.astype(BF).reshape(2, 4, 4, 16, C)

    def sum_block(core, ref, step, x_hi):
        if core == 0:
            return ref.at[:, x_hi, (place.y + step) % 4]
        return ref.at[:, x_hi, :, (place.z + step) % 4]

    def sum_copies(core):
        axis = "y" if core == 0 else "z"
        ahead, behind = place.along(axis, 1), place.along(axis, 3)
        far = [remote(sum_block(core, sent, 2, 0), from_far.at[0], sum_sems, 2, ahead),
               remote(sum_block(core, sent, 2, 1), from_far.at[1], sum_sems, 3, behind)]
        plain = [remote(sum_block(core, sent, 1, 1), from_near.at[0, 1], sum_sems, 4, ahead),
                 remote(sum_block(core, sent, 3, 0), from_near.at[1, 0], sum_sems, 5, behind)]
        summed = [remote(relay.at[0], from_near.at[0, 0], sum_sems, 6, ahead),
                  remote(relay.at[1], from_near.at[1, 1], sum_sems, 7, behind)]
        return far, plain, summed

    def second_copies(core):
        mine = place.z if core == 0 else place.y
        return [remote(sent2.at[:, :, (mine + step) % 4], from_second.at[step - 1], sum_sems, 8 + step - 1,
                       place.along("z" if core == 0 else "y", step)) for step in (1, 2, 3)]

    def sum_start(core):
        far, plain, _ = sum_copies(core)
        for copy in far + plain:
            copy.start()

    def sum_relay(core):
        far, _, summed = sum_copies(core)
        for way, (step, x_hi) in enumerate(((1, 0), (3, 1))):
            far[way].wait()
            relay[way] = (sum_block(core, total, step, x_hi)[...] + from_far[way].astype(F32)).astype(BF)
            summed[way].start()

    def sum_second(core):
        _, plain, summed = sum_copies(core)
        for copy in plain + summed:
            copy.wait()
        for x_hi in range(2):
            added = (sum_block(core, total, 0, x_hi)[...] + from_near[0, x_hi].astype(F32)
                     + from_near[1, x_hi].astype(F32))
            total2[x_hi] = added
            sent2[x_hi] = added.astype(BF)
        for copy in second_copies(core):
            copy.start()

    def sum_third(core):
        for copy in second_copies(core):
            copy.wait()
        added = total2[:, :, place.z if core == 0 else place.y]
        for step in range(3):
            added = added + from_second[step].astype(F32)
        sent3[...] = added.astype(BF)

    @pl.loop(0, 2)
    def _(unit):
        for when, stage in enumerate((sum_start, sum_relay)):
            for core in range(2):
                pl.when((unit == when) & (place.core == core))(functools.partial(stage, core))
        finish(unit)

    both(sum_second)

    @pl.loop(0, SLABS - 1)
    def _(slab):
        store_slab(slab)
        for copy in out_copies(slab):
            copy.start()

    both(sum_third)
    copies = []
    for slot, flips in enumerate(GROUP):
        target = place.x_hi if flips[0] == 0 else 1 - place.x_hi
        copies.append(remote(sent3.at[target], from_group.at[here], final_sems, slot, place.mate(flips)))
    for copy in copies:
        copy.start()
    from_group[here] = sent3[place.x_hi]
    for copy in copies:
        copy.wait()
    position = place.x_lo * 2 + place.core
    for block in range(4):
        added = from_group[0, 0, block // 2, block % 2].astype(F32)
        for a, b in ((0, 1), (1, 0), (1, 1)):
            added = added + from_group[a, b, block // 2, block % 2].astype(F32)
        picked = added[:4]
        for i in range(1, 4):
            picked = jnp.where(position == i, added[4 * i : 4 * i + 4], picked)
        sums_ref[:, C * block : C * (block + 1)] = picked * factor
    for slab in range(SLABS):
        for copy in back_copies(slab):
            copy.wait()
    for slab in range(SLABS - 1):
        for copy in out_copies(slab):
            copy.wait()
    for copy in out_copies_last() + back_copies_last():
        copy.wait()


def fused(latent, cotangent, qkv_weight, out_weight, factor):
    anywhere = pl.BlockSpec(memory_space=pltpu.HBM)
    whole = pl.BlockSpec(memory_space=pltpu.VMEM)
    grid_shape = jax.ShapeDtypeStruct((LEVELS, ROWS, COLS, C), BF)
    dma = pltpu.SemaphoreType.DMA
    return pl.pallas_call(
        functools.partial(fused_kernel, factor),
        out_shape=(
            grid_shape,
            grid_shape,
            jax.ShapeDtypeStruct((2, LEVELS, HALF_ROWS, COLS, C), BF),
            jax.ShapeDtypeStruct((2, LEVELS, TILES, 16, C), BF),
            jax.ShapeDtypeStruct((2, LEVELS, 2, 16, C), BF),
            jax.ShapeDtypeStruct((4, 4 * C), F32),
        ),
        in_specs=[anywhere, anywhere, whole, whole],
        out_specs=(anywhere,) * 5 + (whole,),
        scratch_shapes=[
            pltpu.VMEM((2, LEVELS, ROWS + HALF_ROWS, COLS, C), BF),
            pltpu.VMEM((2, LEVELS, TILES, 16, C), BF),
            pltpu.VMEM((2, LEVELS, 2, 16, C), BF),
            pltpu.VMEM((2, LEVELS, TILES - 1, 16, C), BF),
            pltpu.VMEM((2, LEVELS, 2, 16, C), BF),
            pltpu.VMEM((2, 16, 256), BF),
            pltpu.VMEM((2, 2, 2, 16, 256), BF),
            pltpu.VMEM((2, 2, 64, 128), F32),
            pltpu.VMEM((2, 4, 4, 16, 4 * C), BF),
            pltpu.VMEM((2, PIECES, COLS + 8, C), F32),
            pltpu.VMEM((2, TOK, C), F32),
            pltpu.VMEM((2, TOKENS, C), BF),
            pltpu.VMEM((TOKENS, 1), F32),
            pltpu.VMEM((TOKENS, C), BF),
            pltpu.VMEM((TOKENS, C), BF),
            pltpu.VMEM((SLAB, C), BF),
            pltpu.VMEM((SLAB, 3 * C), BF),
            pltpu.VMEM((2, C, TOKENS), BF),
            pltpu.VMEM((TOKENS, 4 * C), BF),
            pltpu.VMEM((2, TOK, 128), F32),
            pltpu.VMEM((2, TOK, 128), F32),
            pltpu.VMEM((2, LEVELS, TILES, 16, C), BF),
            pltpu.VMEM((2, 2, 4, 4, 16, C), BF),
            pltpu.VMEM((2, 2, 4, 4, 16, C), BF),
            pltpu.VMEM((2, 2, 4, 4, 16, C), F32),
            pltpu.VMEM((2, 2, 4, 4, 16, C), BF),
            pltpu.VMEM((2, 2, 2, 4, 16, C), BF),
            pltpu.VMEM((2, 2, 4, 16, C), BF),
            pltpu.VMEM((2, 2, 4, 16, C), BF),
            pltpu.VMEM((2, 2, 4, 16, C), F32),
            pltpu.VMEM((2, 2, 4, 16, C), BF),
            pltpu.VMEM((3, 2, 2, 16, C), BF),
            pltpu.VMEM((2, 2, 16, C), BF),
            pltpu.VMEM((2, 2, 2, 2, 16, C), BF),
            dma((2,)),
            dma((2, 8)),
            dma((2, 7)),
            dma((2, 9)),
            dma((2, 4)),
            dma((SLABS, 2)),
            dma((2, 12)),
            dma((2, 11)),
            dma((2, 7)),
        ],
        compiler_params=pltpu.CompilerParams(
            collective_id=0, has_side_effects=True, vmem_limit_bytes=62 * 2**20),
        name="layer",
    )(latent, cotangent, qkv_weight, out_weight)


def merge_kernel(
    out_in, grad_in, hr_hbm, hc_hbm, hd_hbm, sums_ref, out_ref, grad_ref, qkv_ref, o_ref,
    grid, hr_ref, hc_ref, hd_ref, load_sems, store_sems,
):
    parts = [(which, level) for which in range(2) for level in range(LEVELS)]
    loads = []
    for which, level in parts:
        loads.append([pltpu.make_async_copy(src.at[which, level], dst.at[which, level], load_sems.at[which, level, i])
                      for i, (src, dst) in enumerate(((hc_hbm, hc_ref), (hd_hbm, hd_ref), (hr_hbm, hr_ref)))])
        own = (out_in, grad_in)[which].at[level, HALF_ROWS:]
        loads[-1].append(pltpu.make_async_copy(own, grid.at[which, level, HALF_ROWS:], load_sems.at[which, level, 3]))
        for load in loads[-1]:
            load.start()
    qkv_ref[...] = sums_ref[:, : 3 * C]
    o_ref[...] = sums_ref[:, 3 * C :]
    column = lax.broadcasted_iota(jnp.int32, (16, C), 0)
    blank = jnp.zeros((8, C), F32)
    stores = []
    for (which, level), coming in zip(parts, loads):
        for load in coming:
            load.wait()
        for row in range(ROWS):
            line = (row - HALF_ROWS) % ROWS
            ref = hc_ref if row >= HALF_ROWS else hd_ref
            tile = line // 2 if row >= HALF_ROWS else line // 2 - (TILES - 2)
            half = line % 2
            halo = jnp.concatenate([ref[which, level, tile].astype(F32)[8 * half : 8 * half + 8], blank], 0)
            own = grid[which, level, row, :16] if row >= HALF_ROWS else hr_ref[which, level, row, :16]
            grid[which, level, row, :16] = jnp.where(column < HALF_COLS, halo, own.astype(F32)).astype(BF)
            if row < HALF_ROWS:
                grid[which, level, row, 16:] = hr_ref[which, level, row, 16:]
        stores.append(pltpu.make_async_copy(grid.at[which, level], (out_ref, grad_ref)[which].at[level],
                                            store_sems.at[which, level]))
        stores[-1].start()
    for store in stores:
        store.wait()


def merge(out, grad, row_strip, col_strip, corner, sums):
    anywhere = pl.BlockSpec(memory_space=pltpu.HBM)
    whole = pl.BlockSpec(memory_space=pltpu.VMEM)
    grid_shape = jax.ShapeDtypeStruct((LEVELS, ROWS, COLS, C), BF)
    return pl.pallas_call(
        merge_kernel,
        out_shape=(grid_shape, grid_shape, jax.ShapeDtypeStruct((4, 3 * C), F32), jax.ShapeDtypeStruct((4, C), F32)),
        in_specs=[anywhere] * 5 + [whole],
        out_specs=(anywhere, anywhere, whole, whole),
        scratch_shapes=[
            pltpu.VMEM((2, LEVELS, ROWS, COLS, C), BF),
            pltpu.VMEM((2, LEVELS, HALF_ROWS, COLS, C), BF),
            pltpu.VMEM((2, LEVELS, TILES, 16, C), BF),
            pltpu.VMEM((2, LEVELS, 2, 16, C), BF),
            pltpu.SemaphoreType.DMA((2, LEVELS, 4)),
            pltpu.SemaphoreType.DMA((2, LEVELS)),
        ],
        compiler_params=pltpu.CompilerParams(vmem_limit_bytes=62 * 2**20),
        name="merge",
    )(out, grad, row_strip, col_strip, corner, sums)


def body(latent, cotangent, qkv_weight, out_weight):
    total_tokens = TOKENS * lax.axis_size("lat") * lax.axis_size("lon")
    done = fused(latent, cotangent, qkv_weight, out_weight, 1.0 / math.sqrt(total_tokens))
    return merge(*done)


def solution(mesh):
    grid = P(None, "lat", "lon", None)
    rows = P(("lat", "lon"), None)
    specs = (grid, grid, rows, rows)
    return jax.shard_map(body, mesh=mesh, in_specs=specs, out_specs=specs, check_vma=False)
```

```python
import functools
import math

import jax
import jax.numpy as jnp
from jax import lax
from jax.experimental import pallas as pl
from jax.experimental.pallas import tpu as pltpu
from jax.sharding import PartitionSpec as P

C = 512
HD = 64
WIN_LAT = 6
WIN_LON = 12
LEVELS = 2
PIECES = LEVELS * WIN_LAT
TOK = PIECES * WIN_LON
SLABS = 4
ACROSS = 4
WINDOWS = SLABS * ACROSS
TOKENS = WINDOWS * TOK
SLAB = ACROSS * TOK
HALF_ROWS = 3
HALF_COLS = 6
ROWS = 24
COLS = 48
TILES = ROWS // 2
HALF = 2 * C
BF = jnp.bfloat16
F32 = jnp.float32


def nn(a, b):
    return lax.dot_general(a, b, (((1,), (0,)), ((), ())), preferred_element_type=F32)


def nt(a, b):
    return lax.dot_general(a, b, (((1,), (1,)), ((), ())), preferred_element_type=F32)


def tn(a, b):
    return lax.dot_general(a, b, (((0,), (0,)), ((), ())), preferred_element_type=F32)


MESH = pl.DeviceIdType.MESH
GROUP = [(a, b, c) for a in range(2) for b in range(2) for c in range(2)][1:]


EDGE_STEP, ROWS_STEP = 3, 2


def first_token(slab, across):
    if isinstance(slab, int) and slab == SLABS - 1:
        return SLAB * ROWS_STEP + TOK * across
    if across == ACROSS - 1:
        return pl.multiple_of(SLAB * EDGE_STEP + TOK * (slab + 1), 16)
    line = 3 * slab + across
    return pl.multiple_of(TOK * (line + line // 8 * 4), 16)


class Place:
    def __init__(self):
        self.lat, self.lon = lax.axis_index("lat"), lax.axis_index("lon")
        self.x_hi, self.y = self.lat // 4, self.lat % 4
        self.z, self.x_lo, self.core = self.lon // 4, (self.lon // 2) % 2, self.lon % 2

    def mate(self, flips):
        a, b, c = (v + f - 2 * v * f for v, f in zip((self.x_hi, self.x_lo, self.core), flips))
        return (a * 4 + self.y, self.z * 4 + b * 2 + c)

    def along(self, axis, step):
        if axis == "y":
            return (self.x_hi * 4 + (self.y + step) % 4, self.lon)
        return (self.lat, (self.z + step) % 4 * 4 + self.lon % 4)

    def shifted(self, rows, cols):
        return ((self.lat + rows + 8) % 8, (self.lon + cols + 16) % 16)


def greet(senders):
    barrier = pltpu.get_barrier_semaphore()
    for device in senders:
        pl.semaphore_signal(barrier, inc=1, device_id=device, device_id_type=MESH)
    pl.semaphore_wait(barrier, len(senders))


def remote(src, dst, sems, slot, device):
    return pltpu.make_async_remote_copy(
        src_ref=src, dst_ref=dst, send_sem=sems.at[0, slot], recv_sem=sems.at[1, slot],
        device_id=device, device_id_type=MESH)


def partners(place):
    return ([place.mate(f) for f in GROUP]
            + [place.along("y", s) for s in (1, 2, 3)] + [place.along("z", s) for s in (1, 2, 3)])


def fused_kernel(
    factor,
    lat_ref, cot_ref, qkv_shard, out_shard,
    out_ref, grad_ref, back_rows, back_cols, back_corner, sums_ref,
    grid, cols_in, corner_in, strip, corner_strip,
    shard_ref, shard_in, loose, weights,
    rows, window, results, inv_w, normed, ctx, gctx, qkv,
    lhs_t, gp, bias, bias_tail,
    cols_out,
    terms, from_mate, total, sent, from_near, from_far, relay, total2, sent2, from_second, sent3, from_group,
    grid_sems, halo_sems, group_sems, axis_sems, mate_sems, out_sems, back_sems, sum_sems, final_sems,
):
    place = Place()
    loads = [pltpu.make_async_copy(ref, grid.at[i, :, :ROWS], grid_sems.at[i]) for i, ref in enumerate((lat_ref, cot_ref))]
    for load in loads:
        load.start()
    near = [place.shifted(1, 0), place.shifted(0, 1), place.shifted(1, 1),
            place.shifted(-1, 0), place.shifted(0, -1), place.shifted(-1, -1)]
    barrier = pltpu.get_barrier_semaphore()
    for device in partners(place) + near:
        pl.semaphore_signal(barrier, inc=1, device_id=device, device_id_type=MESH)
    down, right, across_down, up, left, across_up = near

    def both(stage):
        for core in range(2):
            pl.when(place.core == core)(functools.partial(stage, core))

    for core in range(2):
        for block in range(4):
            for lane_tile in range(2):
                start = HALF * core + 256 * block + 128 * lane_tile
                piece = qkv_shard[:, start : start + 128] if start < 3 * C else out_shard[:, start - 3 * C : start - 3 * C + 128]
                loose[core, lane_tile, pl.ds(block, 4, stride=4)] = piece.astype(F32)
        shard_ref[core] = jnp.concatenate([loose[core, 0, :16], loose[core, 1, :16]], 1).astype(BF)

    pl.semaphore_wait(barrier, len(partners(place)) + len(near))

    here = (place.x_hi, place.x_lo, place.core)
    group = []
    for slot, flips in enumerate(GROUP):
        copy = remote(shard_ref.at[place.core if flips[2] == 0 else 1 - place.core],
                      shard_in.at[here], group_sems, slot, place.mate(flips))
        copy.start()
        group.append(copy)
    shard_in[here] = shard_ref[place.core]

    last = lax.axis_index("lat") == lax.axis_size("lat") - 1
    key = lax.broadcasted_iota(jnp.int32, (TOK, 128), 0)
    query = lax.broadcasted_iota(jnp.int32, (TOK, 128), 1)

    def flag(token):
        row = token // WIN_LON
        return jnp.where(row >= WIN_LAT, row - WIN_LAT, row) >= HALF_ROWS

    seam = jnp.where(last, -1e30, 0.0).astype(F32)
    bias[0] = jnp.zeros((TOK, 128), F32)
    bias_tail[0] = jnp.zeros((TOK, 128), F32)
    bias[1] = jnp.where(flag(key) != flag(query), seam, 0.0)
    bias_tail[1] = jnp.where(flag(key), 0.0, seam)

    for which in range(2):
        loads[which].wait()
        for level in range(LEVELS):
            def columns(row):
                return grid[which, level, row, :16].astype(F32)[:8]
            for tile in range(TILES - 1):
                first = HALF_ROWS + 2 * tile
                strip[which, level, tile] = jnp.concatenate(
                    [columns(first), columns(min(first + 1, ROWS - 1))], 0).astype(BF)
            corner_strip[which, level, 0] = jnp.concatenate([columns(0), columns(0)], 0).astype(BF)
            corner_strip[which, level, 1] = jnp.concatenate([columns(1), columns(2)], 0).astype(BF)
    halo_cols, halo_rows = [], []
    for which in range(2):
        halo_cols.append(remote(strip.at[which], cols_in.at[which, :, : TILES - 1], halo_sems, which, left))
        halo_rows.append(remote(corner_strip.at[which], corner_in.at[which], halo_sems, 2 + which, across_up))
        for level in range(LEVELS):
            halo_rows.append(remote(grid.at[which, level, :HALF_ROWS], grid.at[which, level, ROWS:], halo_sems,
                                    4 + 2 * which + level, up))

    for copy in group:
        copy.wait()
    for x_hi in range(2):
        for b in range(2):
            for c in range(2):
                for lane_tile in range(2):
                    line = 16 * (2 * b + c)
                    loose[x_hi, lane_tile, line : line + 16] = (
                        shard_in[x_hi, b, c][:, 128 * lane_tile : 128 * lane_tile + 128].astype(F32))
    def load_window(slab, across):
        start = HALF_COLS + WIN_LON * across
        low_col, high_col = start // 16 * 16, min(-(-(start + WIN_LON) // 16) * 16, COLS)
        for which in range(2):
            for level in range(LEVELS):
                for row in range(WIN_LAT):
                    piece = level * WIN_LAT + row
                    rows[which, piece, low_col:high_col] = (
                        grid[which, level, slab * WIN_LAT + row + HALF_ROWS, low_col:high_col].astype(F32))
                    if across == ACROSS - 1:
                        half = row % 2
                        rows[which, piece, COLS:] = (
                            cols_in[which, level, 3 * slab + row // 2].astype(F32)[8 * half : 8 * half + 8])
                    window[which, WIN_LON * piece : WIN_LON * (piece + 1)] = rows[which, piece, start : start + WIN_LON]
        part = pl.ds(first_token(slab, across), TOK)
        widened = window[0]
        centred = widened - jnp.mean(widened, -1, keepdims=True)
        inv = lax.rsqrt(jnp.mean(centred * centred, -1, keepdims=True) + 1e-05)
        results[0, part] = widened.astype(BF)
        inv_w[part] = inv
        normed[part] = (centred * inv).astype(BF)
        gp[part, 3 * C :] = window[1].astype(BF)

    def small_copies(core):
        block = weights.at[:, place.y, place.z, :, HALF * core : HALF * (core + 1)]
        return [remote(block, block, axis_sems, step - 1, place.along("z" if core == 0 else "y", step)) for step in (1, 2, 3)]

    def ring_block(core, step, x_hi=slice(None)):
        half = slice(HALF * core, HALF * (core + 1))
        if core == 0:
            return weights.at[x_hi, (place.y + step) % 4, :, :, half]
        return weights.at[x_hi, :, (place.z + step) % 4, :, half]

    def ring_copies(core):
        axis = "y" if core == 0 else "z"
        ahead, behind = place.along(axis, 1), place.along(axis, 3)
        piece = [ring_block(core, 0, 0), ring_block(core, 0, 1)]
        far, near = ring_block(core, 3, 0), ring_block(core, 1, 1)
        return ([remote(piece[i], piece[i], axis_sems, 3 + i, ahead) for i in (0, 1)],
                [remote(piece[i], piece[i], axis_sems, 5 + i, behind) for i in (1, 0)],
                [remote(far, far, axis_sems, 7, ahead), remote(near, near, axis_sems, 8, behind)])

    def mate_copies(core):
        other = place.mate((0, 0, 1))
        return [remote(ring_block(core, step), ring_block(core, step), mate_sems, slot, other)
                for slot, step in enumerate((0, 3, 1, 2))]

    def spread_shards(core):
        for x_hi in range(2):
            for block in range(4):
                for lane_tile in range(2):
                    start = HALF * core + 256 * block + 128 * lane_tile
                    weights[x_hi, place.y, place.z, :, start : start + 128] = (
                        loose[x_hi, lane_tile, pl.ds(block, 16, stride=4)].astype(BF))
        for copy in small_copies(core):
            copy.start()

    def ring_start(core):
        for copy in small_copies(core):
            copy.wait()
        ahead, behind, _ = ring_copies(core)
        for one, other in zip(ahead, behind):
            one.start()
            other.start()
        mate_copies(core)[0].start()

    def ring_relay(core):
        ahead, behind, far = ring_copies(core)
        mates = mate_copies(core)
        ahead[0].wait()
        far[0].start()
        behind[0].wait()
        far[1].start()
        ahead[1].wait()
        behind[1].wait()
        mates[1].start()
        mates[2].start()

    def ring_end(core):
        for copy in ring_copies(core)[2]:
            copy.wait()
        mate_copies(core)[3].start()

    def mates_end(core):
        for copy in mate_copies(core):
            copy.wait()

    @pl.loop(0, SLABS - 1)
    def _(slab):
        for when, stage in enumerate((spread_shards, ring_start, ring_relay)):
            for core in range(2):
                pl.when((slab == when) & (place.core == core))(functools.partial(stage, core))
        for across in range(ACROSS - 1):
            load_window(slab, across)

    both(ring_end)
    for copy in halo_cols + halo_rows:
        copy.start()
    both(mates_end)
    w_ref = weights.reshape(C, 4 * C)

    lane = lax.broadcasted_iota(jnp.int32, (1, 128), 1)
    low = (lane < HD).astype(F32).astype(BF)
    high = (lane >= HD).astype(F32).astype(BF)
    low_lanes = lax.broadcasted_iota(jnp.int32, (128, 128), 1) < HD
    low_lanes16 = lax.broadcasted_iota(jnp.int32, (16, 128), 1) < HD

    def spread(tail):
        zero = jnp.zeros((16, 128), BF)
        lines = []
        for head in range(8):
            pair = head // 2
            mine = tail[:, 128 * pair : 128 * (pair + 1)] * (low if head % 2 == 0 else high)
            lines.append(jnp.concatenate([mine if p == pair else zero for p in range(4)], 1))
        return jnp.concatenate(lines, 0)

    def gather(full, pair):
        cols = slice(128 * pair, 128 * (pair + 1))
        return jnp.where(low_lanes16, full[32 * pair : 32 * pair + 16, cols], full[32 * pair + 16 : 32 * pair + 32, cols])

    def softmax_both(scores, grad_att):
        top = jnp.max(scores, 0, keepdims=True)
        raised = jnp.exp(scores - top)
        att = raised * (1.0 / jnp.sum(raised, 0, keepdims=True))
        weighed = grad_att * att
        inner = jnp.sum(weighed, 0, keepdims=True)
        return att.astype(BF), (weighed - att * inner).astype(BF)

    def attend(base, seam_slab):
        offset = bias[seam_slab]
        offset = jnp.concatenate([offset, offset], 1)
        units = []
        for across in range(ACROSS):
            token = across * TOK
            main, tail, whole = slice(token, token + 128), slice(token + 128, token + TOK), slice(token, token + TOK)
            keys = qkv[whole, C : 2 * C]
            values = qkv[whole, 2 * C :]
            units.append((across, None, spread(qkv[tail, :C]), spread(gctx[tail]), keys, values))
            for pair in range(4):
                cols = slice(128 * pair, 128 * (pair + 1))
                q = qkv[main, cols]
                g = gctx[main, cols]
                q_both = jnp.concatenate([q * low, q * high], 0)
                g_both = jnp.concatenate([g * low, g * high], 0)
                units.append((across, pair, q_both, g_both, keys[:, cols], values[:, cols]))
        products = [(nt(k, q), nt(v, g)) for _, _, q, g, k, v in units]
        softened = []
        for unit, (scores, grad_att) in zip(units, products):
            softened.append(softmax_both(scores + (bias_tail[seam_slab] if unit[1] is None else offset), grad_att))
        made = [(tn(a, v), tn(s, k)) for (a, s), (_, _, q, g, k, v) in zip(softened, units)]
        made2 = [(nn(s, q), nn(a, g)) for (a, s), (_, _, q, g, k, v) in zip(softened, units)]
        for unit, (context, grad_q), (grad_k, grad_v) in zip(units, made, made2):
            across, pair = unit[:2]
            if pair is None:
                ctx_tail, gq_tail, gk_tail, gv_tail = context, grad_q, grad_k, grad_v
                continue
            token = across * TOK
            cols = slice(128 * pair, 128 * (pair + 1))
            g_main = pl.ds(pl.multiple_of(base + token, 16), 128)
            g_tail = pl.ds(pl.multiple_of(base + token + 128, 16), 16)
            g_whole = pl.ds(pl.multiple_of(base + token, 16), TOK)
            ctx[g_main, cols] = jnp.where(low_lanes, context[:128], context[128:]).astype(BF)
            ctx[g_tail, cols] = gather(ctx_tail, pair).astype(BF)
            gp[g_main, cols] = (jnp.where(low_lanes, grad_q[:128], grad_q[128:]) * HD ** -0.5).astype(BF)
            gp[g_tail, cols] = (gather(gq_tail, pair) * HD ** -0.5).astype(BF)
            gp[g_whole, C + 128 * pair : C + 128 * (pair + 1)] = (grad_k + gk_tail[:, cols]).astype(BF)
            gp[g_whole, 2 * C + 128 * pair : 2 * C + 128 * (pair + 1)] = (grad_v + gv_tail[:, cols]).astype(BF)

    def results_to_rows(slab, across):
        part = pl.ds(first_token(slab, across), TOK)
        start = HALF_COLS + WIN_LON * across
        for which in range(2):
            window[which] = results[which, part].astype(F32)
            for piece in range(PIECES):
                rows[which, piece, start : start + WIN_LON] = window[which, WIN_LON * piece : WIN_LON * (piece + 1)]

    def rows_to_strip(slab):
        for which in range(2):
            for level in range(LEVELS):
                for tile in range(3):
                    piece = level * WIN_LAT + 2 * tile
                    cols_out[which, level, 3 * slab + tile] = jnp.concatenate(
                        [rows[which, piece, COLS:], rows[which, piece + 1, COLS:]], 0).astype(BF)

    def store_slab(slab):
        for across in range(ACROSS):
            results_to_rows(slab, across)
        for which in range(2):
            for level in range(LEVELS):
                for row in range(WIN_LAT):
                    grid[which, level, slab * WIN_LAT + row + HALF_ROWS] = rows[which, level * WIN_LAT + row, :COLS].astype(BF)

    def out_copies(slab):
        first = slab * WIN_LAT + HALF_ROWS
        return [pltpu.make_async_copy(grid.at[which, :, pl.ds(first, WIN_LAT)], target.at[:, pl.ds(first, WIN_LAT)], out_sems.at[slab, which])
                for which, target in enumerate((out_ref, grad_ref))]

    def out_copies_last():
        return [pltpu.make_async_copy(grid.at[which, :, ROWS - HALF_ROWS : ROWS], target.at[:, ROWS - HALF_ROWS :],
                                      out_sems.at[SLABS - 1, which])
                for which, target in enumerate((out_ref, grad_ref))]

    def back_copies(slab):
        return [remote(cols_out.at[which, :, pl.ds(3 * slab, 3)], back_cols.at[which, :, pl.ds(3 * slab, 3)], back_sems,
                       2 * slab + which, right) for which in range(2)]

    def back_copies_last():
        copies = []
        for which in range(2):
            copies.append(remote(grid.at[which, :, ROWS:], back_rows.at[which], back_sems, 8 + which, down))
            copies.append(remote(cols_out.at[which, :, TILES - 2 :], back_corner.at[which], back_sems, 10 + which, across_down))
        return copies

    def finish(unit):
        part = pl.ds(pl.multiple_of(unit * SLAB, 64), SLAB)
        results[0, part] = (results[0, part].astype(F32) + nn(ctx[part], w_ref[:, 3 * C :])).astype(BF)
        grad_normed = nt(gp[part, : 3 * C], w_ref[:, : 3 * C])
        standard = normed[part].astype(F32)
        first_mean = jnp.mean(grad_normed, -1, keepdims=True)
        second_mean = jnp.mean(grad_normed * standard, -1, keepdims=True)
        results[1, part] = (inv_w[part] * (grad_normed - first_mean - standard * second_mean)
                            + gp[part, 3 * C :].astype(F32)).astype(BF)

    @pl.loop(0, SLABS)
    def _(step):
        base = pl.multiple_of(step * SLAB, 64)
        part = pl.ds(base, SLAB)

        @pl.when(step == 2)
        def _():
            for copy in halo_cols:
                copy.wait()

        @pl.when(step == EDGE_STEP)
        def _():
            @pl.loop(0, SLABS - 1)
            def _(slab):
                load_window(slab, ACROSS - 1)

        @pl.when(step == ROWS_STEP)
        def _():
            for copy in halo_rows:
                copy.wait()
            for which in range(2):
                for level in range(LEVELS):
                    cols_in[which, level, TILES - 2] = jnp.concatenate(
                        [cols_in[which, level, TILES - 2].astype(F32)[:8], corner_in[which, level, 0].astype(F32)[8:]], 0).astype(BF)
                    cols_in[which, level, TILES - 1] = corner_in[which, level, 1]
            for across in range(ACROSS):
                load_window(SLABS - 1, across)

        block = normed[part]
        for third in range(3):
            cols = slice(C * third, C * (third + 1))
            projected = nn(block, w_ref[:, cols]).astype(BF)
            qkv[:, cols] = projected * BF(HD ** -0.5) if third == 0 else projected
        gctx[...] = nt(gp[part, 3 * C :], w_ref[:, 3 * C :]).astype(BF)
        attend(base, step // 3 if ROWS_STEP == 3 else step // 2 * (1 - step // 3))
        @pl.when(step >= 2)
        def _():
            finish(step)

        @pl.when(step == EDGE_STEP)
        def _():
            @pl.loop(0, SLABS - 1)
            def _(slab):
                results_to_rows(slab, ACROSS - 1)
                rows_to_strip(slab)
                for copy in back_copies(slab):
                    copy.start()

        @pl.when(step == ROWS_STEP)
        def _():
            store_slab(SLABS - 1)
            rows_to_strip(SLABS - 1)
            for copy in back_copies_last() + back_copies(SLABS - 1) + out_copies_last():
                copy.start()

        @pl.when(step % 2 == 1)
        def _():
            two = pl.ds(pl.multiple_of(step // 2 * (2 * SLAB), 128), 2 * SLAB)
            lhs_t[0, :, two] = normed[two].T
            lhs_t[1, :, two] = ctx[two].T

    other = place.mate((0, 0, 1))

    def columns_of(half, part):
        return (half * 2 + part) % 4

    def product(block):
        return nn(lhs_t[block // 3], gp[:, pl.ds(pl.multiple_of(block * C, 128), C)])

    def mate_copy(part):
        return remote(terms.at[part], from_mate.at[part], sum_sems, part, other)

    @pl.loop(0, 2)
    def _(part):
        terms[part] = product(columns_of(1 - place.core, part)).astype(BF).reshape(2, 4, 4, 16, C)
        mate_copy(part).start()

    @pl.loop(0, 2)
    def _(part):
        mate_copy(part).wait()
        added = product(columns_of(place.core, part)) + from_mate[part].reshape(C, C).astype(F32)
        total[part] = added.reshape(2, 4, 4, 16, C)
        sent[part] = added.astype(BF).reshape(2, 4, 4, 16, C)

    def sum_block(core, ref, step, x_hi):
        if core == 0:
            return ref.at[:, x_hi, (place.y + step) % 4]
        return ref.at[:, x_hi, :, (place.z + step) % 4]

    def sum_copies(core):
        axis = "y" if core == 0 else "z"
        ahead, behind = place.along(axis, 1), place.along(axis, 3)
        far = [remote(sum_block(core, sent, 2, 0), from_far.at[0], sum_sems, 2, ahead),
               remote(sum_block(core, sent, 2, 1), from_far.at[1], sum_sems, 3, behind)]
        plain = [remote(sum_block(core, sent, 1, 1), from_near.at[0, 1], sum_sems, 4, ahead),
                 remote(sum_block(core, sent, 3, 0), from_near.at[1, 0], sum_sems, 5, behind)]
        summed = [remote(relay.at[0], from_near.at[0, 0], sum_sems, 6, ahead),
                  remote(relay.at[1], from_near.at[1, 1], sum_sems, 7, behind)]
        return far, plain, summed

    def second_copies(core):
        mine = place.z if core == 0 else place.y
        return [remote(sent2.at[:, :, (mine + step) % 4], from_second.at[step - 1], sum_sems, 8 + step - 1,
                       place.along("z" if core == 0 else "y", step)) for step in (1, 2, 3)]

    def sum_start(core):
        far, plain, _ = sum_copies(core)
        for copy in far + plain:
            copy.start()

    def sum_relay(core):
        far, _, summed = sum_copies(core)
        for way, (step, x_hi) in enumerate(((1, 0), (3, 1))):
            far[way].wait()
            relay[way] = (sum_block(core, total, step, x_hi)[...] + from_far[way].astype(F32)).astype(BF)
            summed[way].start()

    def sum_second(core):
        _, plain, summed = sum_copies(core)
        for copy in plain + summed:
            copy.wait()
        for x_hi in range(2):
            added = (sum_block(core, total, 0, x_hi)[...] + from_near[0, x_hi].astype(F32)
                     + from_near[1, x_hi].astype(F32))
            total2[x_hi] = added
            sent2[x_hi] = added.astype(BF)
        for copy in second_copies(core):
            copy.start()

    def sum_third(core):
        for copy in second_copies(core):
            copy.wait()
        added = total2[:, :, place.z if core == 0 else place.y]
        for step in range(3):
            added = added + from_second[step].astype(F32)
        sent3[...] = added.astype(BF)

    @pl.loop(0, 2)
    def _(unit):
        for when, stage in enumerate((sum_start, sum_relay)):
            for core in range(2):
                pl.when((unit == when) & (place.core == core))(functools.partial(stage, core))
        finish(unit)

    both(sum_second)

    @pl.loop(0, SLABS - 1)
    def _(slab):
        store_slab(slab)
        for copy in out_copies(slab):
            copy.start()

    both(sum_third)
    copies = []
    for slot, flips in enumerate(GROUP):
        target = place.x_hi if flips[0] == 0 else 1 - place.x_hi
        copies.append(remote(sent3.at[target], from_group.at[here], final_sems, slot, place.mate(flips)))
    for copy in copies:
        copy.start()
    from_group[here] = sent3[place.x_hi]
    for copy in copies:
        copy.wait()
    position = place.x_lo * 2 + place.core
    for block in range(4):
        added = from_group[0, 0, block // 2, block % 2].astype(F32)
        for a, b in ((0, 1), (1, 0), (1, 1)):
            added = added + from_group[a, b, block // 2, block % 2].astype(F32)
        picked = added[:4]
        for i in range(1, 4):
            picked = jnp.where(position == i, added[4 * i : 4 * i + 4], picked)
        sums_ref[:, C * block : C * (block + 1)] = picked * factor
    for slab in range(SLABS):
        for copy in back_copies(slab):
            copy.wait()
    for slab in range(SLABS - 1):
        for copy in out_copies(slab):
            copy.wait()
    for copy in out_copies_last() + back_copies_last():
        copy.wait()


def fused(latent, cotangent, qkv_weight, out_weight, factor):
    anywhere = pl.BlockSpec(memory_space=pltpu.HBM)
    whole = pl.BlockSpec(memory_space=pltpu.VMEM)
    grid_shape = jax.ShapeDtypeStruct((LEVELS, ROWS, COLS, C), BF)
    dma = pltpu.SemaphoreType.DMA
    return pl.pallas_call(
        functools.partial(fused_kernel, factor),
        out_shape=(
            grid_shape,
            grid_shape,
            jax.ShapeDtypeStruct((2, LEVELS, HALF_ROWS, COLS, C), BF),
            jax.ShapeDtypeStruct((2, LEVELS, TILES, 16, C), BF),
            jax.ShapeDtypeStruct((2, LEVELS, 2, 16, C), BF),
            jax.ShapeDtypeStruct((4, 4 * C), F32),
        ),
        in_specs=[anywhere, anywhere, whole, whole],
        out_specs=(anywhere,) * 5 + (whole,),
        scratch_shapes=[
            pltpu.VMEM((2, LEVELS, ROWS + HALF_ROWS, COLS, C), BF),
            pltpu.VMEM((2, LEVELS, TILES, 16, C), BF),
            pltpu.VMEM((2, LEVELS, 2, 16, C), BF),
            pltpu.VMEM((2, LEVELS, TILES - 1, 16, C), BF),
            pltpu.VMEM((2, LEVELS, 2, 16, C), BF),
            pltpu.VMEM((2, 16, 256), BF),
            pltpu.VMEM((2, 2, 2, 16, 256), BF),
            pltpu.VMEM((2, 2, 64, 128), F32),
            pltpu.VMEM((2, 4, 4, 16, 4 * C), BF),
            pltpu.VMEM((2, PIECES, COLS + 8, C), F32),
            pltpu.VMEM((2, TOK, C), F32),
            pltpu.VMEM((2, TOKENS, C), BF),
            pltpu.VMEM((TOKENS, 1), F32),
            pltpu.VMEM((TOKENS, C), BF),
            pltpu.VMEM((TOKENS, C), BF),
            pltpu.VMEM((SLAB, C), BF),
            pltpu.VMEM((SLAB, 3 * C), BF),
            pltpu.VMEM((2, C, TOKENS), BF),
            pltpu.VMEM((TOKENS, 4 * C), BF),
            pltpu.VMEM((2, TOK, 128), F32),
            pltpu.VMEM((2, TOK, 128), F32),
            pltpu.VMEM((2, LEVELS, TILES, 16, C), BF),
            pltpu.VMEM((2, 2, 4, 4, 16, C), BF),
            pltpu.VMEM((2, 2, 4, 4, 16, C), BF),
            pltpu.VMEM((2, 2, 4, 4, 16, C), F32),
            pltpu.VMEM((2, 2, 4, 4, 16, C), BF),
            pltpu.VMEM((2, 2, 2, 4, 16, C), BF),
            pltpu.VMEM((2, 2, 4, 16, C), BF),
            pltpu.VMEM((2, 2, 4, 16, C), BF),
            pltpu.VMEM((2, 2, 4, 16, C), F32),
            pltpu.VMEM((2, 2, 4, 16, C), BF),
            pltpu.VMEM((3, 2, 2, 16, C), BF),
            pltpu.VMEM((2, 2, 16, C), BF),
            pltpu.VMEM((2, 2, 2, 2, 16, C), BF),
            dma((2,)),
            dma((2, 8)),
            dma((2, 7)),
            dma((2, 9)),
            dma((2, 4)),
            dma((SLABS, 2)),
            dma((2, 12)),
            dma((2, 11)),
            dma((2, 7)),
        ],
        compiler_params=pltpu.CompilerParams(
            collective_id=0, has_side_effects=True, vmem_limit_bytes=62 * 2**20),
        name="layer",
    )(latent, cotangent, qkv_weight, out_weight)


def merge_kernel(
    out_in, grad_in, hr_hbm, hc_hbm, hd_hbm, sums_ref, out_ref, grad_ref, qkv_ref, o_ref,
    edge, bulk, hr_ref, hc_ref, hd_ref, load_sems, store_sems,
):
    parts = [(which, level) for which in range(2) for level in range(LEVELS)]
    loads, stores = [], []
    for which, level in parts:
        loads.append([pltpu.make_async_copy(src.at[which, level], dst.at[which, level], load_sems.at[which, level, i])
                      for i, (src, dst) in enumerate(((hc_hbm, hc_ref), (hd_hbm, hd_ref), (hr_hbm, hr_ref)))])
        own = (out_in, grad_in)[which].at[level, HALF_ROWS:, :16]
        loads[-1].append(pltpu.make_async_copy(own, edge.at[which, level], load_sems.at[which, level, 3]))
        for load in loads[-1]:
            load.start()
    rests = [pltpu.make_async_copy((out_in, grad_in)[which].at[level, HALF_ROWS:, 16:], bulk.at[which, level],
                                   load_sems.at[which, level, 4]) for which, level in parts]
    for rest in rests:
        rest.start()
    qkv_ref[...] = sums_ref[:, : 3 * C]
    o_ref[...] = sums_ref[:, 3 * C :]
    column = lax.broadcasted_iota(jnp.int32, (16, C), 0)
    blank = jnp.zeros((8, C), F32)
    for (which, level), coming, rest in zip(parts, loads, rests):
        for load in coming:
            load.wait()
        for row in range(ROWS):
            line = (row - HALF_ROWS) % ROWS
            ref = hc_ref if row >= HALF_ROWS else hd_ref
            tile = line // 2 if row >= HALF_ROWS else line // 2 - (TILES - 2)
            half = line % 2
            halo = jnp.concatenate([ref[which, level, tile].astype(F32)[8 * half : 8 * half + 8], blank], 0)
            if row >= HALF_ROWS:
                own = edge[which, level, row - HALF_ROWS].astype(F32)
                edge[which, level, row - HALF_ROWS] = jnp.where(column < HALF_COLS, halo, own).astype(BF)
            else:
                own = hr_ref[which, level, row, :16].astype(F32)
                hr_ref[which, level, row, :16] = jnp.where(column < HALF_COLS, halo, own).astype(BF)
        target = (out_ref, grad_ref)[which]
        stores.append(pltpu.make_async_copy(edge.at[which, level], target.at[level, HALF_ROWS:, :16],
                                            store_sems.at[which, level, 1]))
        stores.append(pltpu.make_async_copy(hr_ref.at[which, level], target.at[level, :HALF_ROWS],
                                            store_sems.at[which, level, 2]))
        rest.wait()
        stores.append(pltpu.make_async_copy(bulk.at[which, level], target.at[level, HALF_ROWS:, 16:],
                                            store_sems.at[which, level, 0]))
        for store in stores[-3:]:
            store.start()
    for store in stores:
        store.wait()


def merge(out, grad, row_strip, col_strip, corner, sums):
    anywhere = pl.BlockSpec(memory_space=pltpu.HBM)
    whole = pl.BlockSpec(memory_space=pltpu.VMEM)
    grid_shape = jax.ShapeDtypeStruct((LEVELS, ROWS, COLS, C), BF)
    return pl.pallas_call(
        merge_kernel,
        out_shape=(grid_shape, grid_shape, jax.ShapeDtypeStruct((4, 3 * C), F32), jax.ShapeDtypeStruct((4, C), F32)),
        in_specs=[anywhere] * 5 + [whole],
        out_specs=(anywhere, anywhere, whole, whole),
        scratch_shapes=[
            pltpu.VMEM((2, LEVELS, ROWS - HALF_ROWS, 16, C), BF),
            pltpu.VMEM((2, LEVELS, ROWS - HALF_ROWS, COLS - 16, C), BF),
            pltpu.VMEM((2, LEVELS, HALF_ROWS, COLS, C), BF),
            pltpu.VMEM((2, LEVELS, TILES, 16, C), BF),
            pltpu.VMEM((2, LEVELS, 2, 16, C), BF),
            pltpu.SemaphoreType.DMA((2, LEVELS, 5)),
            pltpu.SemaphoreType.DMA((2, LEVELS, 3)),
        ],
        compiler_params=pltpu.CompilerParams(vmem_limit_bytes=62 * 2**20),
        name="merge",
    )(out, grad, row_strip, col_strip, corner, sums)


def body(latent, cotangent, qkv_weight, out_weight):
    total_tokens = TOKENS * lax.axis_size("lat") * lax.axis_size("lon")
    done = fused(latent, cotangent, qkv_weight, out_weight, 1.0 / math.sqrt(total_tokens))
    return merge(*done)


def solution(mesh):
    grid = P(None, "lat", "lon", None)
    rows = P(("lat", "lon"), None)
    specs = (grid, grid, rows, rows)
    return jax.shard_map(body, mesh=mesh, in_specs=specs, out_specs=specs, check_vma=False)
```

```python
import functools
import math

import jax
import jax.numpy as jnp
from jax import lax
from jax.experimental import pallas as pl
from jax.experimental.pallas import tpu as pltpu
from jax.sharding import PartitionSpec as P

C = 512
HD = 64
WIN_LAT = 6
WIN_LON = 12
LEVELS = 2
PIECES = LEVELS * WIN_LAT
TOK = PIECES * WIN_LON
SLABS = 4
ACROSS = 4
WINDOWS = SLABS * ACROSS
TOKENS = WINDOWS * TOK
SLAB = ACROSS * TOK
HALF_ROWS = 3
HALF_COLS = 6
ROWS = 24
COLS = 48
TILES = ROWS // 2
HALF = 2 * C
BF = jnp.bfloat16
F32 = jnp.float32


def nn(a, b):
    return lax.dot_general(a, b, (((1,), (0,)), ((), ())), preferred_element_type=F32)


def nt(a, b):
    return lax.dot_general(a, b, (((1,), (1,)), ((), ())), preferred_element_type=F32)


def tn(a, b):
    return lax.dot_general(a, b, (((0,), (0,)), ((), ())), preferred_element_type=F32)


MESH = pl.DeviceIdType.MESH
GROUP = [(a, b, c) for a in range(2) for b in range(2) for c in range(2)][1:]


EDGE_STEP, ROWS_STEP = 3, 2


def first_token(slab, across):
    if isinstance(slab, int) and slab == SLABS - 1:
        return SLAB * ROWS_STEP + TOK * across
    if across == ACROSS - 1:
        return pl.multiple_of(SLAB * EDGE_STEP + TOK * (slab + 1), 16)
    line = 3 * slab + across
    return pl.multiple_of(TOK * (line + line // 8 * 4), 16)


class Place:
    def __init__(self):
        self.lat, self.lon = lax.axis_index("lat"), lax.axis_index("lon")
        self.x_hi, self.y = self.lat // 4, self.lat % 4
        self.z, self.x_lo, self.core = self.lon // 4, (self.lon // 2) % 2, self.lon % 2

    def mate(self, flips):
        a, b, c = (v + f - 2 * v * f for v, f in zip((self.x_hi, self.x_lo, self.core), flips))
        return (a * 4 + self.y, self.z * 4 + b * 2 + c)

    def along(self, axis, step):
        if axis == "y":
            return (self.x_hi * 4 + (self.y + step) % 4, self.lon)
        return (self.lat, (self.z + step) % 4 * 4 + self.lon % 4)

    def shifted(self, rows, cols):
        return ((self.lat + rows + 8) % 8, (self.lon + cols + 16) % 16)


def greet(senders):
    barrier = pltpu.get_barrier_semaphore()
    for device in senders:
        pl.semaphore_signal(barrier, inc=1, device_id=device, device_id_type=MESH)
    pl.semaphore_wait(barrier, len(senders))


def remote(src, dst, sems, slot, device):
    return pltpu.make_async_remote_copy(
        src_ref=src, dst_ref=dst, send_sem=sems.at[0, slot], recv_sem=sems.at[1, slot],
        device_id=device, device_id_type=MESH)


def partners(place):
    return ([place.mate(f) for f in GROUP]
            + [place.along("y", s) for s in (1, 2, 3)] + [place.along("z", s) for s in (1, 2, 3)])


def fused_kernel(
    factor,
    lat_ref, cot_ref, qkv_shard, out_shard,
    out_ref, grad_ref, back_rows, back_cols, back_corner, sums_ref,
    grid, cols_in, corner_in, strip, corner_strip,
    shard_ref, shard_in, loose, weights,
    rows, window, results, inv_w, normed, ctx, gctx, qkv,
    lhs_t, gp, bias, bias_tail,
    cols_out,
    terms, from_mate, total, sent, from_near, from_far, relay, total2, sent2, from_second, sent3, from_group,
    grid_sems, halo_sems, group_sems, axis_sems, mate_sems, out_sems, back_sems, sum_sems, final_sems,
):
    place = Place()
    loads = [pltpu.make_async_copy(ref, grid.at[i, :, :ROWS], grid_sems.at[i]) for i, ref in enumerate((lat_ref, cot_ref))]
    for load in loads:
        load.start()
    near = [place.shifted(1, 0), place.shifted(0, 1), place.shifted(1, 1),
            place.shifted(-1, 0), place.shifted(0, -1), place.shifted(-1, -1)]
    barrier = pltpu.get_barrier_semaphore()
    for device in partners(place) + near:
        pl.semaphore_signal(barrier, inc=1, device_id=device, device_id_type=MESH)
    down, right, across_down, up, left, across_up = near

    def both(stage):
        for core in range(2):
            pl.when(place.core == core)(functools.partial(stage, core))

    for core in range(2):
        for block in range(4):
            for lane_tile in range(2):
                start = HALF * core + 256 * block + 128 * lane_tile
                piece = qkv_shard[:, start : start + 128] if start < 3 * C else out_shard[:, start - 3 * C : start - 3 * C + 128]
                loose[core, lane_tile, pl.ds(block, 4, stride=4)] = piece.astype(F32)
        shard_ref[core] = jnp.concatenate([loose[core, 0, :16], loose[core, 1, :16]], 1).astype(BF)

    pl.semaphore_wait(barrier, len(partners(place)) + len(near))

    here = (place.x_hi, place.x_lo, place.core)
    group = []
    for slot, flips in enumerate(GROUP):
        copy = remote(shard_ref.at[place.core if flips[2] == 0 else 1 - place.core],
                      shard_in.at[here], group_sems, slot, place.mate(flips))
        copy.start()
        group.append(copy)
    shard_in[here] = shard_ref[place.core]

    last = lax.axis_index("lat") == lax.axis_size("lat") - 1
    key = lax.broadcasted_iota(jnp.int32, (TOK, 128), 0)
    query = lax.broadcasted_iota(jnp.int32, (TOK, 128), 1)

    def flag(token):
        row = token // WIN_LON
        return jnp.where(row >= WIN_LAT, row - WIN_LAT, row) >= HALF_ROWS

    seam = jnp.where(last, -1e30, 0.0).astype(F32)
    bias[0] = jnp.zeros((TOK, 128), F32)
    bias_tail[0] = jnp.zeros((TOK, 128), F32)
    bias[1] = jnp.where(flag(key) != flag(query), seam, 0.0)
    bias_tail[1] = jnp.where(flag(key), 0.0, seam)

    for which in range(2):
        loads[which].wait()
        for level in range(LEVELS):
            def columns(row):
                return grid[which, level, row, :16].astype(F32)[:8]
            for tile in range(TILES - 1):
                first = HALF_ROWS + 2 * tile
                strip[which, level, tile] = jnp.concatenate(
                    [columns(first), columns(min(first + 1, ROWS - 1))], 0).astype(BF)
            corner_strip[which, level, 0] = jnp.concatenate([columns(0), columns(0)], 0).astype(BF)
            corner_strip[which, level, 1] = jnp.concatenate([columns(1), columns(2)], 0).astype(BF)
    halo_cols, halo_rows = [], []
    for which in range(2):
        halo_cols.append(remote(strip.at[which], cols_in.at[which, :, : TILES - 1], halo_sems, which, left))
        halo_rows.append(remote(corner_strip.at[which], corner_in.at[which], halo_sems, 2 + which, across_up))
        for level in range(LEVELS):
            halo_rows.append(remote(grid.at[which, level, :HALF_ROWS], grid.at[which, level, ROWS:], halo_sems,
                                    4 + 2 * which + level, up))

    for copy in group:
        copy.wait()
    for x_hi in range(2):
        for b in range(2):
            for c in range(2):
                for lane_tile in range(2):
                    line = 16 * (2 * b + c)
                    loose[x_hi, lane_tile, line : line + 16] = (
                        shard_in[x_hi, b, c][:, 128 * lane_tile : 128 * lane_tile + 128].astype(F32))
    def load_window(slab, across):
        start = HALF_COLS + WIN_LON * across
        low_col, high_col = start // 16 * 16, min(-(-(start + WIN_LON) // 16) * 16, COLS)
        for which in range(2):
            for level in range(LEVELS):
                for row in range(WIN_LAT):
                    piece = level * WIN_LAT + row
                    rows[which, piece, low_col:high_col] = (
                        grid[which, level, slab * WIN_LAT + row + HALF_ROWS, low_col:high_col].astype(F32))
                    if across == ACROSS - 1:
                        half = row % 2
                        rows[which, piece, COLS:] = (
                            cols_in[which, level, 3 * slab + row // 2].astype(F32)[8 * half : 8 * half + 8])
                    window[which, WIN_LON * piece : WIN_LON * (piece + 1)] = rows[which, piece, start : start + WIN_LON]
        part = pl.ds(first_token(slab, across), TOK)
        widened = window[0]
        centred = widened - jnp.mean(widened, -1, keepdims=True)
        inv = lax.rsqrt(jnp.mean(centred * centred, -1, keepdims=True) + 1e-05)
        results[0, part] = widened.astype(BF)
        inv_w[part] = inv
        normed[part] = (centred * inv).astype(BF)
        gp[part, 3 * C :] = window[1].astype(BF)

    def small_copies(core):
        block = weights.at[:, place.y, place.z, :, HALF * core : HALF * (core + 1)]
        return [remote(block, block, axis_sems, step - 1, place.along("z" if core == 0 else "y", step)) for step in (1, 2, 3)]

    def ring_block(core, step, x_hi=slice(None)):
        half = slice(HALF * core, HALF * (core + 1))
        if core == 0:
            return weights.at[x_hi, (place.y + step) % 4, :, :, half]
        return weights.at[x_hi, :, (place.z + step) % 4, :, half]

    def ring_copies(core):
        axis = "y" if core == 0 else "z"
        ahead, behind = place.along(axis, 1), place.along(axis, 3)
        piece = [ring_block(core, 0, 0), ring_block(core, 0, 1)]
        far, near = ring_block(core, 3, 0), ring_block(core, 1, 1)
        return ([remote(piece[i], piece[i], axis_sems, 3 + i, ahead) for i in (0, 1)],
                [remote(piece[i], piece[i], axis_sems, 5 + i, behind) for i in (1, 0)],
                [remote(far, far, axis_sems, 7, ahead), remote(near, near, axis_sems, 8, behind)])

    def mate_copies(core):
        other = place.mate((0, 0, 1))
        return [remote(ring_block(core, step), ring_block(core, step), mate_sems, slot, other)
                for slot, step in enumerate((0, 3, 1, 2))]

    def spread_shards(core):
        for x_hi in range(2):
            for block in range(4):
                for lane_tile in range(2):
                    start = HALF * core + 256 * block + 128 * lane_tile
                    weights[x_hi, place.y, place.z, :, start : start + 128] = (
                        loose[x_hi, lane_tile, pl.ds(block, 16, stride=4)].astype(BF))
        for copy in small_copies(core):
            copy.start()

    def ring_start(core):
        for copy in small_copies(core):
            copy.wait()
        ahead, behind, _ = ring_copies(core)
        for one, other in zip(ahead, behind):
            one.start()
            other.start()
        mate_copies(core)[0].start()

    def ring_relay(core):
        ahead, behind, far = ring_copies(core)
        mates = mate_copies(core)
        ahead[0].wait()
        far[0].start()
        behind[0].wait()
        far[1].start()
        ahead[1].wait()
        behind[1].wait()
        mates[1].start()
        mates[2].start()

    def ring_end(core):
        for copy in ring_copies(core)[2]:
            copy.wait()
        mate_copies(core)[3].start()

    def mates_end(core):
        for copy in mate_copies(core):
            copy.wait()

    @pl.loop(0, SLABS - 1)
    def _(slab):
        for when, stage in enumerate((spread_shards, ring_start, ring_relay)):
            for core in range(2):
                pl.when((slab == when) & (place.core == core))(functools.partial(stage, core))
        for across in range(ACROSS - 1):
            load_window(slab, across)

    both(ring_end)
    for copy in halo_cols + halo_rows:
        copy.start()
    both(mates_end)
    w_ref = weights.reshape(C, 4 * C)

    lane = lax.broadcasted_iota(jnp.int32, (1, 128), 1)
    low = (lane < HD).astype(F32).astype(BF)
    high = (lane >= HD).astype(F32).astype(BF)
    low_lanes = lax.broadcasted_iota(jnp.int32, (128, 128), 1) < HD
    low_lanes16 = lax.broadcasted_iota(jnp.int32, (16, 128), 1) < HD

    def spread(tail):
        zero = jnp.zeros((16, 128), BF)
        lines = []
        for head in range(8):
            pair = head // 2
            mine = tail[:, 128 * pair : 128 * (pair + 1)] * (low if head % 2 == 0 else high)
            lines.append(jnp.concatenate([mine if p == pair else zero for p in range(4)], 1))
        return jnp.concatenate(lines, 0)

    def gather(full, pair):
        cols = slice(128 * pair, 128 * (pair + 1))
        return jnp.where(low_lanes16, full[32 * pair : 32 * pair + 16, cols], full[32 * pair + 16 : 32 * pair + 32, cols])

    def softmax_both(scores, grad_att):
        top = jnp.max(scores, 0, keepdims=True)
        raised = jnp.exp(scores - top)
        att = raised * (1.0 / jnp.sum(raised, 0, keepdims=True))
        weighed = grad_att * att
        inner = jnp.sum(weighed, 0, keepdims=True)
        return att.astype(BF), (weighed - att * inner).astype(BF)

    def attend(base, seam_slab):
        offset = bias[seam_slab]
        offset = jnp.concatenate([offset, offset], 1)
        units = []
        for across in range(ACROSS):
            token = across * TOK
            main, tail, whole = slice(token, token + 128), slice(token + 128, token + TOK), slice(token, token + TOK)
            keys = qkv[whole, C : 2 * C]
            values = qkv[whole, 2 * C :]
            units.append((across, None, spread(qkv[tail, :C]), spread(gctx[tail]), keys, values))
            for pair in range(4):
                cols = slice(128 * pair, 128 * (pair + 1))
                q = qkv[main, cols]
                g = gctx[main, cols]
                q_both = jnp.concatenate([q * low, q * high], 0)
                g_both = jnp.concatenate([g * low, g * high], 0)
                units.append((across, pair, q_both, g_both, keys[:, cols], values[:, cols]))
        products = [(nt(k, q), nt(v, g)) for _, _, q, g, k, v in units]
        softened = []
        for unit, (scores, grad_att) in zip(units, products):
            softened.append(softmax_both(scores + (bias_tail[seam_slab] if unit[1] is None else offset), grad_att))
        made = [(tn(a, v), tn(s, k)) for (a, s), (_, _, q, g, k, v) in zip(softened, units)]
        made2 = [(nn(s, q), nn(a, g)) for (a, s), (_, _, q, g, k, v) in zip(softened, units)]
        for unit, (context, grad_q), (grad_k, grad_v) in zip(units, made, made2):
            across, pair = unit[:2]
            if pair is None:
                ctx_tail, gq_tail, gk_tail, gv_tail = context, grad_q, grad_k, grad_v
                continue
            token = across * TOK
            cols = slice(128 * pair, 128 * (pair + 1))
            g_main = pl.ds(pl.multiple_of(base + token, 16), 128)
            g_tail = pl.ds(pl.multiple_of(base + token + 128, 16), 16)
            g_whole = pl.ds(pl.multiple_of(base + token, 16), TOK)
            ctx[g_main, cols] = jnp.where(low_lanes, context[:128], context[128:]).astype(BF)
            ctx[g_tail, cols] = gather(ctx_tail, pair).astype(BF)
            gp[g_main, cols] = (jnp.where(low_lanes, grad_q[:128], grad_q[128:]) * HD ** -0.5).astype(BF)
            gp[g_tail, cols] = (gather(gq_tail, pair) * HD ** -0.5).astype(BF)
            gp[g_whole, C + 128 * pair : C + 128 * (pair + 1)] = (grad_k + gk_tail[:, cols]).astype(BF)
            gp[g_whole, 2 * C + 128 * pair : 2 * C + 128 * (pair + 1)] = (grad_v + gv_tail[:, cols]).astype(BF)

    def results_to_rows(slab, across):
        part = pl.ds(first_token(slab, across), TOK)
        start = HALF_COLS + WIN_LON * across
        for which in range(2):
            window[which] = results[which, part].astype(F32)
            for piece in range(PIECES):
                rows[which, piece, start : start + WIN_LON] = window[which, WIN_LON * piece : WIN_LON * (piece + 1)]

    def rows_to_strip(slab):
        for which in range(2):
            for level in range(LEVELS):
                for tile in range(3):
                    piece = level * WIN_LAT + 2 * tile
                    cols_out[which, level, 3 * slab + tile] = jnp.concatenate(
                        [rows[which, piece, COLS:], rows[which, piece + 1, COLS:]], 0).astype(BF)

    def store_slab(slab):
        for across in range(ACROSS):
            results_to_rows(slab, across)
        for which in range(2):
            for level in range(LEVELS):
                for row in range(WIN_LAT):
                    grid[which, level, slab * WIN_LAT + row + HALF_ROWS] = rows[which, level * WIN_LAT + row, :COLS].astype(BF)

    def out_copies(slab):
        first = slab * WIN_LAT + HALF_ROWS
        return [pltpu.make_async_copy(grid.at[which, :, pl.ds(first, WIN_LAT)], target.at[:, pl.ds(first, WIN_LAT)], out_sems.at[slab, which])
                for which, target in enumerate((out_ref, grad_ref))]

    def out_copies_last():
        return [pltpu.make_async_copy(grid.at[which, :, ROWS - HALF_ROWS : ROWS], target.at[:, ROWS - HALF_ROWS :],
                                      out_sems.at[SLABS - 1, which])
                for which, target in enumerate((out_ref, grad_ref))]

    def back_copies(slab):
        return [remote(cols_out.at[which, :, pl.ds(3 * slab, 3)], back_cols.at[which, :, pl.ds(3 * slab, 3)], back_sems,
                       2 * slab + which, right) for which in range(2)]

    def back_copies_last():
        copies = []
        for which in range(2):
            copies.append(remote(grid.at[which, :, ROWS:], back_rows.at[which], back_sems, 8 + which, down))
            copies.append(remote(cols_out.at[which, :, TILES - 2 :], back_corner.at[which], back_sems, 10 + which, across_down))
        return copies

    def finish(unit):
        part = pl.ds(pl.multiple_of(unit * SLAB, 64), SLAB)
        results[0, part] = (results[0, part].astype(F32) + nn(ctx[part], w_ref[:, 3 * C :])).astype(BF)
        grad_normed = nt(gp[part, : 3 * C], w_ref[:, : 3 * C])
        standard = normed[part].astype(F32)
        first_mean = jnp.mean(grad_normed, -1, keepdims=True)
        second_mean = jnp.mean(grad_normed * standard, -1, keepdims=True)
        results[1, part] = (inv_w[part] * (grad_normed - first_mean - standard * second_mean)
                            + gp[part, 3 * C :].astype(F32)).astype(BF)

    @pl.loop(0, SLABS)
    def _(step):
        base = pl.multiple_of(step * SLAB, 64)
        part = pl.ds(base, SLAB)

        @pl.when(step == 2)
        def _():
            for copy in halo_cols:
                copy.wait()

        @pl.when(step == EDGE_STEP)
        def _():
            @pl.loop(0, SLABS - 1)
            def _(slab):
                load_window(slab, ACROSS - 1)

        @pl.when(step == ROWS_STEP)
        def _():
            for copy in halo_rows:
                copy.wait()
            for which in range(2):
                for level in range(LEVELS):
                    cols_in[which, level, TILES - 2] = jnp.concatenate(
                        [cols_in[which, level, TILES - 2].astype(F32)[:8], corner_in[which, level, 0].astype(F32)[8:]], 0).astype(BF)
                    cols_in[which, level, TILES - 1] = corner_in[which, level, 1]
            for across in range(ACROSS):
                load_window(SLABS - 1, across)

        block = normed[part]
        for third in range(3):
            cols = slice(C * third, C * (third + 1))
            projected = nn(block, w_ref[:, cols]).astype(BF)
            qkv[:, cols] = projected * BF(HD ** -0.5) if third == 0 else projected
        gctx[...] = nt(gp[part, 3 * C :], w_ref[:, 3 * C :]).astype(BF)
        attend(base, step // 3 if ROWS_STEP == 3 else step // 2 * (1 - step // 3))
        @pl.when(step >= 2)
        def _():
            finish(step)

        @pl.when(step == EDGE_STEP)
        def _():
            @pl.loop(0, SLABS - 1)
            def _(slab):
                results_to_rows(slab, ACROSS - 1)
                rows_to_strip(slab)
                for copy in back_copies(slab):
                    copy.start()

        @pl.when(step == ROWS_STEP)
        def _():
            store_slab(SLABS - 1)
            rows_to_strip(SLABS - 1)
            for copy in back_copies_last() + back_copies(SLABS - 1) + out_copies_last():
                copy.start()

        @pl.when(step % 2 == 1)
        def _():
            two = pl.ds(pl.multiple_of(step // 2 * (2 * SLAB), 128), 2 * SLAB)
            lhs_t[0, :, two] = normed[two].T
            lhs_t[1, :, two] = ctx[two].T

    other = place.mate((0, 0, 1))

    def columns_of(half, part):
        return (half * 2 + part) % 4

    def product(block):
        return nn(lhs_t[block // 3], gp[:, pl.ds(pl.multiple_of(block * C, 128), C)])

    def mate_copy(part):
        return remote(terms.at[part], from_mate.at[part], sum_sems, part, other)

    @pl.loop(0, 2)
    def _(part):
        terms[part] = product(columns_of(1 - place.core, part)).astype(BF).reshape(2, 4, 4, 16, C)
        mate_copy(part).start()

    @pl.loop(0, 2)
    def _(part):
        mate_copy(part).wait()
        added = product(columns_of(place.core, part)) + from_mate[part].reshape(C, C).astype(F32)
        total[part] = added.reshape(2, 4, 4, 16, C)
        sent[part] = added.astype(BF).reshape(2, 4, 4, 16, C)

    def sum_block(core, ref, step, x_hi):
        if core == 0:
            return ref.at[:, x_hi, (place.y + step) % 4]
        return ref.at[:, x_hi, :, (place.z + step) % 4]

    def sum_copies(core):
        axis = "y" if core == 0 else "z"
        ahead, behind = place.along(axis, 1), place.along(axis, 3)
        far = [remote(sum_block(core, sent, 2, 0), from_far.at[0], sum_sems, 2, ahead),
               remote(sum_block(core, sent, 2, 1), from_far.at[1], sum_sems, 3, behind)]
        plain = [remote(sum_block(core, sent, 1, 1), from_near.at[0, 1], sum_sems, 4, ahead),
                 remote(sum_block(core, sent, 3, 0), from_near.at[1, 0], sum_sems, 5, behind)]
        summed = [remote(relay.at[0], from_near.at[0, 0], sum_sems, 6, ahead),
                  remote(relay.at[1], from_near.at[1, 1], sum_sems, 7, behind)]
        return far, plain, summed

    def second_copies(core):
        mine = place.z if core == 0 else place.y
        return [remote(sent2.at[:, :, (mine + step) % 4], from_second.at[step - 1], sum_sems, 8 + step - 1,
                       place.along("z" if core == 0 else "y", step)) for step in (1, 2, 3)]

    def sum_start(core):
        far, plain, _ = sum_copies(core)
        for copy in far + plain:
            copy.start()

    def sum_relay(core):
        far, _, summed = sum_copies(core)
        for way, (step, x_hi) in enumerate(((1, 0), (3, 1))):
            far[way].wait()
            relay[way] = (sum_block(core, total, step, x_hi)[...] + from_far[way].astype(F32)).astype(BF)
            summed[way].start()

    def sum_second(core):
        _, plain, summed = sum_copies(core)
        for copy in plain + summed:
            copy.wait()
        for x_hi in range(2):
            added = (sum_block(core, total, 0, x_hi)[...] + from_near[0, x_hi].astype(F32)
                     + from_near[1, x_hi].astype(F32))
            total2[x_hi] = added
            sent2[x_hi] = added.astype(BF)
        for copy in second_copies(core):
            copy.start()

    def sum_third(core):
        for copy in second_copies(core):
            copy.wait()
        added = total2[:, :, place.z if core == 0 else place.y]
        for step in range(3):
            added = added + from_second[step].astype(F32)
        sent3[...] = added.astype(BF)

    @pl.loop(0, 2)
    def _(unit):
        for when, stage in enumerate((sum_start, sum_relay)):
            for core in range(2):
                pl.when((unit == when) & (place.core == core))(functools.partial(stage, core))
        finish(unit)

    both(sum_second)

    @pl.loop(0, SLABS - 1)
    def _(slab):
        store_slab(slab)
        for copy in out_copies(slab):
            copy.start()

    both(sum_third)
    copies = []
    for slot, flips in enumerate(GROUP):
        target = place.x_hi if flips[0] == 0 else 1 - place.x_hi
        copies.append(remote(sent3.at[target], from_group.at[here], final_sems, slot, place.mate(flips)))
    for copy in copies:
        copy.start()
    from_group[here] = sent3[place.x_hi]
    for copy in copies:
        copy.wait()
    position = place.x_lo * 2 + place.core
    for block in range(4):
        added = from_group[0, 0, block // 2, block % 2].astype(F32)
        for a, b in ((0, 1), (1, 0), (1, 1)):
            added = added + from_group[a, b, block // 2, block % 2].astype(F32)
        picked = added[:4]
        for i in range(1, 4):
            picked = jnp.where(position == i, added[4 * i : 4 * i + 4], picked)
        sums_ref[:, C * block : C * (block + 1)] = picked * factor
    for slab in range(SLABS):
        for copy in back_copies(slab):
            copy.wait()
    for slab in range(SLABS - 1):
        for copy in out_copies(slab):
            copy.wait()
    for copy in out_copies_last() + back_copies_last():
        copy.wait()


def fused(latent, cotangent, qkv_weight, out_weight, factor):
    anywhere = pl.BlockSpec(memory_space=pltpu.HBM)
    whole = pl.BlockSpec(memory_space=pltpu.VMEM)
    grid_shape = jax.ShapeDtypeStruct((LEVELS, ROWS, COLS, C), BF)
    dma = pltpu.SemaphoreType.DMA
    return pl.pallas_call(
        functools.partial(fused_kernel, factor),
        out_shape=(
            grid_shape,
            grid_shape,
            jax.ShapeDtypeStruct((2, LEVELS, HALF_ROWS, COLS, C), BF),
            jax.ShapeDtypeStruct((2, LEVELS, TILES, 16, C), BF),
            jax.ShapeDtypeStruct((2, LEVELS, 2, 16, C), BF),
            jax.ShapeDtypeStruct((4, 4 * C), F32),
        ),
        in_specs=[anywhere, anywhere, whole, whole],
        out_specs=(anywhere,) * 5 + (whole,),
        scratch_shapes=[
            pltpu.VMEM((2, LEVELS, ROWS + HALF_ROWS, COLS, C), BF),
            pltpu.VMEM((2, LEVELS, TILES, 16, C), BF),
            pltpu.VMEM((2, LEVELS, 2, 16, C), BF),
            pltpu.VMEM((2, LEVELS, TILES - 1, 16, C), BF),
            pltpu.VMEM((2, LEVELS, 2, 16, C), BF),
            pltpu.VMEM((2, 16, 256), BF),
            pltpu.VMEM((2, 2, 2, 16, 256), BF),
            pltpu.VMEM((2, 2, 64, 128), F32),
            pltpu.VMEM((2, 4, 4, 16, 4 * C), BF),
            pltpu.VMEM((2, PIECES, COLS + 8, C), F32),
            pltpu.VMEM((2, TOK, C), F32),
            pltpu.VMEM((2, TOKENS, C), BF),
            pltpu.VMEM((TOKENS, 1), F32),
            pltpu.VMEM((TOKENS, C), BF),
            pltpu.VMEM((TOKENS, C), BF),
            pltpu.VMEM((SLAB, C), BF),
            pltpu.VMEM((SLAB, 3 * C), BF),
            pltpu.VMEM((2, C, TOKENS), BF),
            pltpu.VMEM((TOKENS, 4 * C), BF),
            pltpu.VMEM((2, TOK, 128), F32),
            pltpu.VMEM((2, TOK, 128), F32),
            pltpu.VMEM((2, LEVELS, TILES, 16, C), BF),
            pltpu.VMEM((2, 2, 4, 4, 16, C), BF),
            pltpu.VMEM((2, 2, 4, 4, 16, C), BF),
            pltpu.VMEM((2, 2, 4, 4, 16, C), F32),
            pltpu.VMEM((2, 2, 4, 4, 16, C), BF),
            pltpu.VMEM((2, 2, 2, 4, 16, C), BF),
            pltpu.VMEM((2, 2, 4, 16, C), BF),
            pltpu.VMEM((2, 2, 4, 16, C), BF),
            pltpu.VMEM((2, 2, 4, 16, C), F32),
            pltpu.VMEM((2, 2, 4, 16, C), BF),
            pltpu.VMEM((3, 2, 2, 16, C), BF),
            pltpu.VMEM((2, 2, 16, C), BF),
            pltpu.VMEM((2, 2, 2, 2, 16, C), BF),
            dma((2,)),
            dma((2, 8)),
            dma((2, 7)),
            dma((2, 9)),
            dma((2, 4)),
            dma((SLABS, 2)),
            dma((2, 12)),
            dma((2, 11)),
            dma((2, 7)),
        ],
        compiler_params=pltpu.CompilerParams(
            collective_id=0, has_side_effects=True, vmem_limit_bytes=62 * 2**20),
        name="layer",
    )(latent, cotangent, qkv_weight, out_weight)


def merge_kernel(
    out_in, grad_in, hr_hbm, hc_hbm, hd_hbm, sums_ref, out_ref, grad_ref, qkv_ref, o_ref,
    edge, bulk, hr_ref, hc_ref, hd_ref, load_sems, store_sems,
):
    parts = [(which, level) for which in range(2) for level in range(LEVELS)]
    loads, stores = [], []
    for which, level in parts:
        loads.append([pltpu.make_async_copy(src.at[which, level], dst.at[which, level], load_sems.at[which, level, i])
                      for i, (src, dst) in enumerate(((hc_hbm, hc_ref), (hd_hbm, hd_ref), (hr_hbm, hr_ref)))])
        own = (out_in, grad_in)[which].at[level, HALF_ROWS:, :16]
        loads[-1].append(pltpu.make_async_copy(own, edge.at[which, level], load_sems.at[which, level, 3]))
    rests = [pltpu.make_async_copy((out_in, grad_in)[which].at[level, HALF_ROWS:, 16:], bulk.at[which, level],
                                   load_sems.at[which, level, 4]) for which, level in parts]
    for coming, rest in zip(loads, rests):
        coming.append(rest)
    for coming in loads[:2]:
        for load in coming:
            load.start()
    qkv_ref[...] = sums_ref[:, : 3 * C]
    o_ref[...] = sums_ref[:, 3 * C :]
    column = lax.broadcasted_iota(jnp.int32, (16, C), 0)
    blank = jnp.zeros((8, C), F32)
    for number, ((which, level), coming) in enumerate(zip(parts, loads)):
        for load in coming:
            load.wait()
        for load in loads[number + 2] if number + 2 < len(loads) else ():
            load.start()
        for row in range(ROWS):
            line = (row - HALF_ROWS) % ROWS
            ref = hc_ref if row >= HALF_ROWS else hd_ref
            tile = line // 2 if row >= HALF_ROWS else line // 2 - (TILES - 2)
            half = line % 2
            halo = jnp.concatenate([ref[which, level, tile].astype(F32)[8 * half : 8 * half + 8], blank], 0)
            if row >= HALF_ROWS:
                own = edge[which, level, row - HALF_ROWS].astype(F32)
                edge[which, level, row - HALF_ROWS] = jnp.where(column < HALF_COLS, halo, own).astype(BF)
            else:
                own = hr_ref[which, level, row, :16].astype(F32)
                hr_ref[which, level, row, :16] = jnp.where(column < HALF_COLS, halo, own).astype(BF)
        target = (out_ref, grad_ref)[which]
        stores.append(pltpu.make_async_copy(edge.at[which, level], target.at[level, HALF_ROWS:, :16],
                                            store_sems.at[which, level, 1]))
        stores.append(pltpu.make_async_copy(hr_ref.at[which, level], target.at[level, :HALF_ROWS],
                                            store_sems.at[which, level, 2]))
        stores.append(pltpu.make_async_copy(bulk.at[which, level], target.at[level, HALF_ROWS:, 16:],
                                            store_sems.at[which, level, 0]))
        for store in stores[-3:]:
            store.start()
    for store in stores:
        store.wait()


def merge(out, grad, row_strip, col_strip, corner, sums):
    anywhere = pl.BlockSpec(memory_space=pltpu.HBM)
    whole = pl.BlockSpec(memory_space=pltpu.VMEM)
    grid_shape = jax.ShapeDtypeStruct((LEVELS, ROWS, COLS, C), BF)
    return pl.pallas_call(
        merge_kernel,
        out_shape=(grid_shape, grid_shape, jax.ShapeDtypeStruct((4, 3 * C), F32), jax.ShapeDtypeStruct((4, C), F32)),
        in_specs=[anywhere] * 5 + [whole],
        out_specs=(anywhere, anywhere, whole, whole),
        scratch_shapes=[
            pltpu.VMEM((2, LEVELS, ROWS - HALF_ROWS, 16, C), BF),
            pltpu.VMEM((2, LEVELS, ROWS - HALF_ROWS, COLS - 16, C), BF),
            pltpu.VMEM((2, LEVELS, HALF_ROWS, COLS, C), BF),
            pltpu.VMEM((2, LEVELS, TILES, 16, C), BF),
            pltpu.VMEM((2, LEVELS, 2, 16, C), BF),
            pltpu.SemaphoreType.DMA((2, LEVELS, 5)),
            pltpu.SemaphoreType.DMA((2, LEVELS, 3)),
        ],
        compiler_params=pltpu.CompilerParams(vmem_limit_bytes=62 * 2**20),
        name="merge",
    )(out, grad, row_strip, col_strip, corner, sums)


def body(latent, cotangent, qkv_weight, out_weight):
    total_tokens = TOKENS * lax.axis_size("lat") * lax.axis_size("lon")
    done = fused(latent, cotangent, qkv_weight, out_weight, 1.0 / math.sqrt(total_tokens))
    return merge(*done)


def solution(mesh):
    grid = P(None, "lat", "lon", None)
    rows = P(("lat", "lon"), None)
    specs = (grid, grid, rows, rows)
    return jax.shard_map(body, mesh=mesh, in_specs=specs, out_specs=specs, check_vma=False)
```
